32 devices in a mesh: scan: 2 (over x), tile: 16 (over z, y, core).
Axes of the slice: x: 2, y: 2, z: 4, core: 2. Of those that a mesh axis runs over, the one named last changes fastest.
Arguments:
- slices: float32 [4, 2, 1024, 1024], P(None, None, ('scan', 'tile')), parts along dimension 2, may hold values from -4 to 4
- probe_modes: float32 [4, 2, 128, 128], P('scan'), parts along dimension 0, may hold values from -4 to 4
- row_offset: int32 [128], P(('scan', 'tile')), parts along dimension 0, may hold values from 0 to 31, as said below
- col_offset: int32 [128], P(('scan', 'tile')), parts along dimension 0, may hold values from 0 to 1023
- amplitude: float32 [128, 128, 128], P(('scan', 'tile')), parts along dimension 0, may hold values from 0.5 to 3
Outputs:
- slice_grad: float32 [4, 2, 1024, 1024], P(None, None, ('scan', 'tile')), parts along dimension 2
- probe_grad: float32 [4, 2, 128, 128], P('scan'), parts along dimension 0
The draws below stay inside these ranges and needn't reach their ends.
There are 2 independent parts, one for each index of `scan`. The reference program is written for one: setup_inputs(seed, part) draws one part's arguments, and reference() takes and returns one part's arrays. A program takes and returns all parts, laid end to end along the dimension named above; each array names one. Nothing has to cross between parts.
Inputs may be any that keep to these rules, and one draw needn't show every extreme that they name: Window w starts 32 * (w // 4) + row_offset[w] rows down the object; the largest value is taken by some window in every draw.
All inputs are finite; a program needn't handle non-finite values.
Results may differ from the reference program's by a relative error of at most 0.0003.
Values sent between devices are 32-bit elements; how exact they have to be, the bound alone decides.
No kernel may reach another device: no remote copies, remote signals or barrier semaphores. Data moves between devices by JAX's collectives and lax.ppermute only.
A program may use at most 128 MiB of HBM per device.

```python
import math
import jax
import jax.numpy as jnp
from jax import lax

W = 128
MODES = 2
SLICES = 4
COLS = 1024
WIN_DEV = 4
ROWS_DEV = 32
NROWS = 512
WINDOWS = 64


def draw_row_offset(key, part):
    values = jax.random.randint(jax.random.fold_in(key, 11), (WINDOWS,), 0, ROWS_DEV, dtype=jnp.int32)
    spot_index = jax.random.randint(jax.random.fold_in(key, 12), (), 0, WINDOWS, dtype=jnp.int32)
    positions = jnp.arange(WINDOWS, dtype=jnp.int32)
    return jnp.where(positions == spot_index, ROWS_DEV - 1, values).astype(jnp.int32)


def set_ends(array, own_key, smallest, top_value):
    extent = array.shape
    place = [jax.random.randint(jax.random.fold_in(own_key, axis), (), 0, extent[axis]) for axis in range(len(extent))]
    array = array.at[tuple(place)].set(smallest)
    longest = extent.index(max(extent))
    place[longest] = (place[longest] + 1) % extent[longest]
    return array.at[tuple(place)].set(top_value)


def block_levels(stream_key, extent, cuts, low, top_value):
    loudness, own = 1.0, jax.random.fold_in(stream_key, 6)
    for dim, shards_of in cuts:
        heights = jnp.exp(jax.random.uniform(jax.random.fold_in(own, dim), (shards_of,), jnp.float32, low / len(cuts), top_value / len(cuts)))
        loudness = loudness * jnp.repeat(heights, extent[dim] // shards_of).reshape([-1 if axis == dim else 1 for axis in range(len(extent))])
    return loudness


def centred(rng, shape, scale, bound, cuts=(), kind=jnp.bfloat16):
    result = jax.random.normal(rng, shape, jnp.float32) * scale
    if len(cuts) > 0:
        result = block_levels(rng, shape, cuts, -0.22, 0.18) * result
    return jnp.clip(result, min=-bound, max=bound).astype(kind)


def setup_inputs(seed: int = 0, part: int = 0) -> dict:
    arg_keys = jax.random.split(jax.random.key(seed), 6)
    own_keys = jax.random.split(jax.random.fold_in(arg_keys[5], part), 6)
    slices = centred(own_keys[0], (SLICES, 2, NROWS, COLS), 0.7, 4.0, ((2, 16),), jnp.float32)
    probe_modes = centred(own_keys[1], (MODES, 2, W, W), 0.7, 4.0, (), jnp.float32)
    row_offset = draw_row_offset(jax.random.fold_in(jax.random.fold_in(arg_keys[5], part), 71), part)
    col_offset = set_ends(jax.random.randint(own_keys[3], (WINDOWS,), 0, COLS), jax.random.fold_in(own_keys[3], 1), 0, COLS - 1).astype(jnp.int32)
    amplitude = jnp.clip(jnp.exp(math.log(3.0) - 1.7917595 * jax.random.uniform(own_keys[4], (WINDOWS, W, W), jnp.float32) ** block_levels(own_keys[4], (WINDOWS, W, W), ((0, 16),), -0.2, 0.2)), 0.5, 3.0)
    return {"slices": slices, "probe_modes": probe_modes, "row_offset": row_offset, "col_offset": col_offset, "amplitude": amplitude}


INTENSITY_SHIFT = 0.5
FRESNEL = 0.75

def dft_tables(window_side):
    steps_idx = jnp.arange(window_side, dtype=jnp.int32)
    product = steps_idx[:, None] * steps_idx[None, :] % window_side
    angles = product.astype(jnp.float32) * (-2.0 * math.pi / window_side)
    scale = 1.0 / math.sqrt(window_side)
    return (jnp.cos(angles) * scale, jnp.sin(angles) * scale)

def fresnel_kernel(window_side):
    steps_idx = jnp.arange(window_side, dtype=jnp.int32)
    freqs = (steps_idx + window_side // 2) % window_side - window_side // 2
    radius = (freqs[:, None] * freqs[:, None] + freqs[None, :] * freqs[None, :]).astype(jnp.float32)
    phase = radius * (-math.pi * FRESNEL / (window_side / 2.0) ** 2)
    return (jnp.cos(phase), jnp.sin(phase))

def left_apply(mat_real, mat_imag, wave_real, wave_imag):

    def product(matrix, field):
        return jnp.einsum('jk,mkl->mjl', matrix, field, precision=lax.Precision.HIGHEST)
    return (product(mat_real, wave_real) - product(mat_imag, wave_imag), product(mat_real, wave_imag) + product(mat_imag, wave_real))

def right_apply(wave_real, wave_imag, mat_real, mat_imag):

    def product(field, matrix):
        return jnp.einsum('mjk,kl->mjl', field, matrix, precision=lax.Precision.HIGHEST)
    return (product(wave_real, mat_real) - product(wave_imag, mat_imag), product(wave_imag, mat_real) + product(wave_real, mat_imag))

def transform(wave_real, wave_imag, mat_real, mat_imag):
    half_real, half_imag = left_apply(mat_real, mat_imag, wave_real, wave_imag)
    return right_apply(half_real, half_imag, mat_real, mat_imag)

def propagate(wave_real, wave_imag, tables):
    cos_table, sin_table, kernel_real, kernel_imag = tables
    spec_real, spec_imag = transform(wave_real, wave_imag, cos_table, sin_table)
    moved_real = spec_real * kernel_real - spec_imag * kernel_imag
    moved_imag = spec_real * kernel_imag + spec_imag * kernel_real
    return transform(moved_real, moved_imag, cos_table, -sin_table)

def window_loss(crops, probe_modes, measured, tables):
    cos_table, sin_table = (tables[0], tables[1])
    wave_real = probe_modes[:, 0]
    wave_imag = probe_modes[:, 1]
    slice_count = crops.shape[0]
    exit_real = wave_real
    exit_imag = wave_imag
    for depth_index in range(slice_count):
        trans_real = crops[depth_index, 0]
        trans_imag = crops[depth_index, 1]
        exit_real = trans_real * wave_real - trans_imag * wave_imag
        exit_imag = trans_real * wave_imag + trans_imag * wave_real
        if depth_index + 1 < slice_count:
            wave_real, wave_imag = propagate(exit_real, exit_imag, tables)
    far_real, far_imag = transform(exit_real, exit_imag, cos_table, sin_table)
    intensity = lax.optimization_barrier(jnp.sum(far_real * far_real + far_imag * far_imag, axis=0))
    modelled = jnp.sqrt(intensity + INTENSITY_SHIFT)
    return 0.5 * jnp.sum((modelled - measured) ** 2)

def window_grads(crops, probe_modes, measured, tables):
    return jax.grad(window_loss, argnums=(0, 1))(crops, probe_modes, measured, tables)

def reference(slices, probe_modes, row_offset, col_offset, amplitude):
    window_side = probe_modes.shape[-1]
    total_rows = slices.shape[2]
    total_cols = slices.shape[3]
    cos_table, sin_table = dft_tables(window_side)
    kernel_real, kernel_imag = fresnel_kernel(window_side)
    tables = (cos_table, sin_table, kernel_real, kernel_imag)
    wrapped = jnp.concatenate([slices, slices[:, :, :window_side - 1]], axis=2)
    wrapped = jnp.concatenate([wrapped, wrapped[:, :, :, :window_side - 1]], axis=3)
    owners = jnp.arange(WINDOWS, dtype=jnp.int32) // WIN_DEV
    row_starts = (owners * ROWS_DEV + row_offset).astype(jnp.int32)
    anchor = jnp.zeros((), jnp.int32)

    def visit(state, inputs):
        slice_acc, probe_acc = state
        row_start, col_start, measured = inputs
        corner = (anchor, anchor, row_start.astype(jnp.int32), col_start.astype(jnp.int32))
        crops = lax.dynamic_slice(wrapped, corner, (SLICES, 2, window_side, window_side))
        crop_grad, probe_term = window_grads(crops, probe_modes, measured, tables)
        current = lax.dynamic_slice(slice_acc, corner, (SLICES, 2, window_side, window_side))
        slice_acc = lax.dynamic_update_slice(slice_acc, current + crop_grad, corner)
        return ((slice_acc, probe_acc + probe_term), None)
    initial = (jnp.zeros(wrapped.shape, jnp.float32), jnp.zeros(probe_modes.shape, jnp.float32))
    (slice_acc, probe_grad), _ = lax.scan(visit, initial, (row_starts, col_offset, amplitude))
    folded = slice_acc[:, :, :total_rows].at[:, :, :window_side - 1].add(slice_acc[:, :, total_rows:])
    folded = folded[:, :, :, :total_cols].at[:, :, :, :window_side - 1].add(folded[:, :, :, total_cols:])
    return (folded, probe_grad)
```

```python
import functools
import math

import numpy as np
import ml_dtypes
import jax
import jax.numpy as jnp
from jax import lax
from jax.experimental import pallas as pl
from jax.experimental.pallas import tpu as pltpu
from jax.sharding import PartitionSpec as P

INTENSITY_SHIFT = 0.5
FRESNEL = 0.75
LANES = 128
VMEM_BYTES = 56 * 1024 * 1024


def pairs(value):
    first = value.astype(ml_dtypes.bfloat16)
    second = (value - first.astype(np.float64)).astype(ml_dtypes.bfloat16)
    return np.stack([first, second])


def real_form(matrix):
    return np.block([[matrix.real, matrix.imag], [-matrix.imag, matrix.real]])


def tables_of(window_side):
    steps = np.arange(window_side)
    angles = -2.0 * math.pi / window_side * (steps[:, None] * steps[None, :] % window_side)
    transform = np.exp(1j * angles) / math.sqrt(window_side)
    freqs = (steps + window_side // 2) % window_side - window_side // 2
    phase = np.exp(-1j * math.pi * FRESNEL * freqs**2 / (window_side / 2.0) ** 2)
    step = transform.conj() @ (phase[:, None] * transform)
    forms = [real_form(m) for m in (step, step.conj(), transform, transform.conj())]
    return np.stack([pairs(form) for form in forms])


def halves(value):
    first = value.astype(jnp.bfloat16)
    return first, (value - first.astype(jnp.float32)).astype(jnp.bfloat16)


def product(left, right):
    return jnp.dot(left, right, preferred_element_type=jnp.float32)


def right_apply(field, table):
    first, second = halves(field)
    return product(first, table[0]) + (product(second, table[0]) + product(first, table[1]))


def left_apply(table, field):
    first, second = halves(field)
    return product(table[0], first) + (product(table[0], second) + product(table[1], first))


def both_sides(waves, right_table, left_table):
    side = waves[0][0].shape[0]
    rows = jnp.concatenate([jnp.concatenate(wave, axis=1) for wave in waves], axis=0)
    half = right_apply(rows, right_table)
    count = len(waves)
    parts = [
        jnp.concatenate(
            [half[m * side : (m + 1) * side, c * side : (c + 1) * side] for m in range(count)], axis=1
        )
        for c in range(2)
    ]
    full = left_apply(left_table, jnp.concatenate(parts, axis=0))
    return [
        tuple(full[c * side : (c + 1) * side, m * side : (m + 1) * side] for c in range(2))
        for m in range(count)
    ]


def times(a, b):
    return (a[0] * b[0] - a[1] * b[1], a[0] * b[1] + a[1] * b[0])


def conj_times(a, b):
    return (a[0] * b[0] + a[1] * b[1], a[0] * b[1] - a[1] * b[0])


def gradient_kernel(group, offset_ref, probe_ref, amplitude_ref, table_ref, *refs):
    count = len(refs) // 2
    pieces, grads, probe_grad_ref = refs[:count], refs[count : 2 * count], refs[2 * count]
    windows, slice_count, _, rows_here, side = pieces[0].shape
    modes = probe_ref.shape[0]
    step, step_conj, transform, transform_conj = (
        (table_ref[i, 0], table_ref[i, 1]) for i in range(4)
    )
    flag = offset_ref[2, 0]
    probe_grad_ref[...] = jnp.zeros(probe_grad_ref.shape, jnp.float32)

    def start(w):
        row, lane = offset_ref[0, w], offset_ref[1, w] % side
        index = lax.broadcasted_iota(jnp.int32, (rows_here, side), 0)
        here = jnp.where(index >= row, 1, 0) != flag
        return row, lane, here

    def crop(w, s, here):
        def plane(c):
            edge = jnp.where(here, pieces[0][w, s, c], pieces[1][w, s, c])
            return jnp.concatenate([edge] + [piece[w, s, c] for piece in pieces[2:]], axis=0)

        return (plane(0), plane(1))

    def keep(w, s, here, grad):
        for c in range(2):
            edge = grad[c][:rows_here]
            zero = jnp.zeros_like(edge)
            grads[0][w, s, c] = jnp.where(here, edge, zero)
            grads[1][w, s, c] = jnp.where(here, zero, edge)
            for j in range(1, count - 1):
                grads[j + 1][w, s, c] = grad[c][j * rows_here : (j + 1) * rows_here]

    def turn(value, row, lane):
        return pltpu.roll(pltpu.roll(value, row, 0), lane, 1)

    def visit(index, carry):
        ids = [index * group + k for k in range(group)]
        places = [start(w) for w in ids]
        waves = [
            [[tuple(turn(probe_ref[m, c], row, lane) for c in range(2)) for m in range(modes)]]
            for row, lane, _ in places
        ]
        crops = [[] for _ in ids]
        exits = [None] * group
        for s in range(slice_count):
            for k, w in enumerate(ids):
                crops[k].append(crop(w, s, places[k][2]))
                exits[k] = [times(crops[k][s], wave) for wave in waves[k][s]]
            for k, w in enumerate(ids):
                if s + 1 < slice_count:
                    waves[k].append(both_sides(exits[k], step, step_conj))
                else:
                    exits[k] = both_sides(exits[k], transform, transform_conj)
        for k, w in enumerate(ids):
            intensity = sum(re * re + im * im for re, im in exits[k])
            scale = 1.0 - amplitude_ref[w] * lax.rsqrt(intensity + INTENSITY_SHIFT)
            exits[k] = [(re * scale, im * scale) for re, im in exits[k]]
        for k, w in enumerate(ids):
            exits[k] = both_sides(exits[k], transform_conj, transform)
        for s in reversed(range(slice_count)):
            for k, w in enumerate(ids):
                terms = [conj_times(wave, out) for wave, out in zip(waves[k][s], exits[k])]
                keep(w, s, places[k][2], [sum(term[c] for term in terms) for c in range(2)])
                exits[k] = [conj_times(crops[k][s], out) for out in exits[k]]
            if s > 0:
                for k, w in enumerate(ids):
                    exits[k] = both_sides(exits[k], step_conj, step)
        for k, (row, lane, _) in enumerate(places):
            for m in range(modes):
                for c in range(2):
                    back = turn(exits[k][m][c], (side - row) % side, (side - lane) % side)
                    probe_grad_ref[m, c] += back
        return carry

    lax.fori_loop(0, windows // group, visit, 0)


def take_kernel(col_ref, slices_ref, *outs):
    blocks = slices_ref.shape[-1] // LANES
    windows = outs[0].shape[0]
    lanes = lax.broadcasted_iota(jnp.int32, (1, 1, 1, LANES), 3)
    for k, out in enumerate(outs):
        for w in range(windows):
            col = col_ref[k, w]
            block, lane = col // LANES, col % LANES
            after = (block + 1) % blocks
            near = slices_ref[:, :, :, pl.ds(pl.multiple_of(block * LANES, LANES), LANES)]
            far = slices_ref[:, :, :, pl.ds(pl.multiple_of(after * LANES, LANES), LANES)]
            out[w] = jnp.where(lanes < lane, far, near)


def give_kernel(col_ref, *refs):
    pieces, out_ref = refs[:-1], refs[-1]
    blocks = out_ref.shape[-1] // LANES
    windows = pieces[0].shape[0]
    lanes = lax.broadcasted_iota(jnp.int32, (1, 1, 1, LANES), 3)
    out_ref[...] = jnp.zeros(out_ref.shape, jnp.float32)
    for k, piece in enumerate(pieces):
        for w in range(windows):
            col = col_ref[k, w]
            block, lane = col // LANES, col % LANES
            after = (block + 1) % blocks
            value = piece[w]
            near = pl.ds(pl.multiple_of(block * LANES, LANES), LANES)
            far = pl.ds(pl.multiple_of(after * LANES, LANES), LANES)
            wraps = lanes < lane
            out_ref[:, :, :, near] += jnp.where(wraps, 0.0, value)
            out_ref[:, :, :, far] += jnp.where(wraps, value, 0.0)


def plan_of(count, reach):
    pair = reach // 2
    if pair == 0 or count % (2 * pair) != 0:
        moved = [0] * count
    else:
        moved = [t // pair % 2 for t in range(count)]
    home = [(t + reach) % count if moved[t] else t for t in range(count)]
    return moved, home


def whole(memory_space=pltpu.VMEM):
    return pl.BlockSpec(memory_space=memory_space)


def call(kernel, outs, args, flops=0):
    smem, vmem = whole(pltpu.SMEM), whole()
    return pl.pallas_call(
        kernel,
        out_shape=outs,
        in_specs=[smem] + [vmem] * (len(args) - 1),
        out_specs=[vmem] * len(outs) if isinstance(outs, list) else vmem,
        compiler_params=pltpu.CompilerParams(vmem_limit_bytes=VMEM_BYTES),
    )(*args)


def all_sum(value, axis):
    count = lax.axis_size(axis)
    if count & (count - 1):
        return lax.psum(value, axis)
    bit = 1
    while bit < count:
        value = value + lax.ppermute(value, axis, [(i, i ^ bit) for i in range(count)])
        bit *= 2
    return value


def on_device(slices, probe_modes, row_offset, col_offset, amplitude):
    side = probe_modes.shape[-1]
    slice_count, _, rows_here, cols = slices.shape
    windows = row_offset.shape[0]
    count = lax.axis_size("tile")
    assert side == LANES and side % rows_here == 0 and cols % LANES == 0
    reach = side // rows_here
    moved, home = plan_of(count, reach)
    me = lax.axis_index("tile")
    is_moved = jnp.asarray(moved, jnp.int32)[me]

    def edge_pairs():
        return [(t, home[t]) if moved[t] else ((t + reach) % count, t) for t in range(count)]

    def inner_pairs(j):
        return [((t + j) % count, home[t]) for t in range(count)]

    def back(pairs_there):
        return [(b, a) for a, b in pairs_there]

    def send(value, pairs_there):
        return lax.ppermute(value, "tile", pairs_there)

    offsets = jnp.stack([row_offset, col_offset])
    behind = [offsets] + [
        send(offsets, [(t, (t + j) % count) for t in range(count)]) for j in range(1, reach + 1)
    ]
    mine = jnp.where(is_moved == 1, behind[reach], offsets)
    other = jnp.where(is_moved == 1, offsets, behind[reach])
    cols_of = jnp.stack([mine[1], other[1]] + [behind[j][1] for j in range(1, reach)])
    rows_of = jnp.concatenate([mine, jnp.full((1, windows), is_moved, jnp.int32)])

    piece = jax.ShapeDtypeStruct((windows, slice_count, 2, rows_here, side), jnp.float32)
    sent = call(take_kernel, [piece] * (reach + 1), (cols_of, slices))
    pieces = [sent[0], send(sent[1], edge_pairs())]
    pieces += [send(sent[j + 1], inner_pairs(j)) for j in range(1, reach)]
    if any(moved):
        amplitude = send(amplitude, list(enumerate(home)))

    tables = jnp.asarray(tables_of(side))
    group = 2 if windows % 2 == 0 else 1
    results = call(
        functools.partial(gradient_kernel, group),
        [piece] * (reach + 1) + [jax.ShapeDtypeStruct(probe_modes.shape, jnp.float32)],
        (rows_of, probe_modes, amplitude, tables, *pieces),
    )
    grads, probe_grad = results[:-1], results[-1]
    received = [grads[0], send(grads[1], back(edge_pairs()))]
    received += [send(grads[j + 1], back(inner_pairs(j))) for j in range(1, reach)]
    own_grad = call(
        give_kernel, jax.ShapeDtypeStruct(slices.shape, jnp.float32), (cols_of, *received)
    )
    return own_grad, all_sum(probe_grad, "tile")


def solution(mesh):
    placed = (
        P(None, None, ("scan", "tile"), None),
        P("scan", None, None, None),
        P(("scan", "tile")),
        P(("scan", "tile")),
        P(("scan", "tile"), None, None),
    )
    return jax.shard_map(
        on_device,
        mesh=mesh,
        in_specs=placed,
        out_specs=(P(None, None, ("scan", "tile"), None), P("scan", None, None, None)),
        check_vma=False,
    )
```

```python
import functools
import math

import numpy as np
import ml_dtypes
import jax
import jax.numpy as jnp
from jax import lax
from jax.experimental import pallas as pl
from jax.experimental.pallas import tpu as pltpu
from jax.sharding import PartitionSpec as P

INTENSITY_SHIFT = 0.5
FRESNEL = 0.75
LANES = 128
VMEM_BYTES = 20 * 1024 * 1024
EXTRA = 8


def pairs(value):
    first = value.astype(ml_dtypes.bfloat16)
    second = (value - first.astype(np.float64)).astype(ml_dtypes.bfloat16)
    return np.stack([first, second])


def real_form(matrix):
    return np.block([[matrix.real, matrix.imag], [-matrix.imag, matrix.real]])


def tables_of(window_side):
    steps = np.arange(window_side)
    angles = -2.0 * math.pi / window_side * (steps[:, None] * steps[None, :] % window_side)
    transform = np.exp(1j * angles) / math.sqrt(window_side)
    freqs = (steps + window_side // 2) % window_side - window_side // 2
    phase = np.exp(-1j * math.pi * FRESNEL * freqs**2 / (window_side / 2.0) ** 2)
    step = transform.conj() @ (phase[:, None] * transform)
    forms = [real_form(m) for m in (step, step.conj(), transform, transform.conj())]
    return np.stack([pairs(form) for form in forms])


def halves(value):
    first = value.astype(jnp.bfloat16)
    return first, (value - first.astype(jnp.float32)).astype(jnp.bfloat16)


def product(left, right):
    return jnp.dot(left, right, preferred_element_type=jnp.float32)


def right_apply(field, table):
    first, second = halves(field)
    return product(first, table[0]) + (product(second, table[0]) + product(first, table[1]))


def left_apply(table, field):
    first, second = halves(field)
    return product(table[0], first) + (product(table[0], second) + product(table[1], first))


def both_sides(waves, right_table, left_table):
    side = waves[0][0].shape[0]
    rows = jnp.concatenate([jnp.concatenate(wave, axis=1) for wave in waves], axis=0)
    half = right_apply(rows, right_table)
    count = len(waves)
    parts = [
        jnp.concatenate(
            [half[m * side : (m + 1) * side, c * side : (c + 1) * side] for m in range(count)], axis=1
        )
        for c in range(2)
    ]
    full = left_apply(left_table, jnp.concatenate(parts, axis=0))
    return [
        tuple(full[c * side : (c + 1) * side, m * side : (m + 1) * side] for c in range(2))
        for m in range(count)
    ]


def times(a, b):
    return (a[0] * b[0] - a[1] * b[1], a[0] * b[1] + a[1] * b[0])


def conj_times(a, b):
    return (a[0] * b[0] + a[1] * b[1], a[0] * b[1] - a[1] * b[0])


class Stage:
    def __init__(self, forward, far, backward, sizes):
        self.forward, self.far, self.backward = forward, far, backward
        self.windows, self.modes, self.side, self.rows_here, self.cols = sizes
        self.reach = self.side // self.rows_here
        self.carry = 0 in backward
        self.grad_rows = self.windows * len(backward) * 2 * self.rows_here
        self.group = math.gcd(self.windows, 4)
        loaded = set(backward) - set(forward)
        waves = loaded | set(forward[:1])
        vmem = ["tables"]
        vmem += ["probe"] if 0 in waves else []
        vmem += ["amplitude"] if far else []
        vmem += [f"psi{s}" for s in sorted(waves) if s > 0] + [f"crop{s}" for s in sorted(loaded)]
        vmem += [] if far else [f"exit{s + 1}" for s in backward[:1]]
        if forward:
            vmem += ["own", "own_mate", "partner", "partner_mate", "edge", "edge_mate", "first_rows"]
        self.vmem_in = vmem
        outs = [f"grad{j}" for j in range(self.reach + 1)] if backward else []
        if not backward:
            outs += [f"psi{s + 1}" for s in forward] + [f"crop{s}" for s in forward]
        else:
            outs.append("part" if self.carry else f"exit{backward[-1]}")
        self.vmem_out = outs
        if backward:
            outs += [f"grad{j}" for j in range(self.reach + 1)]

    def out_shape(self, name):
        side = self.side
        if name.startswith("grad"):
            shape = (self.grad_rows + (EXTRA if self.carry else 0), side)
        elif name == "part":
            shape = (2 * self.modes * side, side)
        elif name.startswith("crop"):
            shape = (self.windows, 2, side, side)
        else:
            shape = (self.windows, self.modes, 2, side, side)
        return jax.ShapeDtypeStruct(shape, jnp.float32)

    def __call__(self, values):
        inputs = ["offsets"] + self.vmem_in
        outputs = self.vmem_out
        args = [values[name] for name in inputs]
        shapes = [self.out_shape(name) for name in outputs]
        smem, vmem = (pl.BlockSpec(memory_space=space) for space in (pltpu.SMEM, pltpu.VMEM))
        outs = pl.pallas_call(
            self.kernel,
            out_shape=shapes,
            in_specs=[smem] + [vmem] * len(self.vmem_in),
            out_specs=[vmem] * len(self.vmem_out),
            cost_estimate=pl.CostEstimate(flops=0, bytes_accessed=0, transcendentals=0),
            compiler_params=pltpu.CompilerParams(vmem_limit_bytes=VMEM_BYTES),
        )(*args)
        return dict(zip(outputs, outs))

    def kernel(self, *refs):
        names = ["offsets"] + self.vmem_in + self.vmem_out
        r = dict(zip(names, refs))
        side, rows_here, modes, group = self.side, self.rows_here, self.modes, self.group
        forward, backward = self.forward, self.backward
        step, step_conj, transform, transform_conj = (
            (r["tables"][i, 0], r["tables"][i, 1]) for i in range(4)
        )
        me = lax.axis_index("tile")
        parity, moved = me % 2, moved_here(me)
        blocks = self.cols // LANES

        if self.carry:
            index = lax.broadcasted_iota(jnp.int32, (EXTRA, side), 0)
            carried = jnp.zeros((EXTRA, side), jnp.int32)
            for w in range(self.windows):
                carried = jnp.where(index == w, r["offsets"][1, w], carried)
            for j in range(1, self.reach + 1):
                r[f"grad{j}"][pl.ds(self.grad_rows, EXTRA)] = carried.astype(jnp.float32)
            r["part"][...] = jnp.zeros(r["part"].shape, jnp.float32)
        def start(w):
            row, col = r["offsets"][0, w], r["offsets"][1, w]
            block = col // LANES
            after = jnp.where(block + 1 == blocks, 0, block + 1)
            near, far = (pl.ds(pl.multiple_of(b * LANES, LANES), LANES) for b in (block, after))
            lane = col % LANES
            below = lax.broadcasted_iota(jnp.int32, (rows_here, side), 0) >= row
            here = jnp.where(below, 1, 0) != moved
            wraps = lax.broadcasted_iota(jnp.int32, (rows_here, side), 1) < lane
            return row, lane, near, far, here, wraps

        def crop(s, place):
            _, _, near, far, here, wraps = place

            def columns(name, c):
                tile = r[name].at[pl.ds((2 * s + c) * rows_here, rows_here)]
                return jnp.where(wraps, tile[:, far], tile[:, near])

            def plane(c):
                first = jnp.where(here, columns("own", c), columns("edge", c))
                outer = jnp.where(parity == moved, columns("own_mate", c), columns("edge_mate", c))
                inner = columns("partner_mate", c)
                pair = [jnp.where(parity == 0, a, b) for a, b in ((outer, inner), (inner, outer))]
                return jnp.concatenate([first, pair[0], columns("partner", c), pair[1]], axis=0)

            return (plane(0), plane(1))

        def keep(w, i, place, grad):
            here = place[4]
            for c in range(2):
                first = ((w * len(backward) + i) * 2 + c) * rows_here
                at = pl.ds(pl.multiple_of(first, rows_here), rows_here)
                rows = [grad[c][j * rows_here : (j + 1) * rows_here] for j in range(self.reach)]
                r["grad0"][at] = jnp.where(here, rows[0], 0.0)
                r["grad1"][at] = jnp.where(here, 0.0, rows[0])
                r["grad2"][at] = rows[2]
                r["grad3"][at] = jnp.where(parity == 0, rows[3], rows[1])
                r["grad4"][at] = jnp.where(parity == 0, rows[1], rows[3])

        def turn(value, row, lane):
            return pltpu.roll(pltpu.roll(value, row, 0), lane, 1)

        def load(ref, w):
            return [tuple(ref[w, m, c] for c in range(2)) for m in range(modes)]

        def store(ref, w, waves):
            for m in range(modes):
                for c in range(2):
                    ref[w, m, c] = waves[m][c]

        def entry(w, s, place):
            if s > 0:
                return load(r[f"psi{s}"], w)
            return [
                tuple(turn(r["probe"][m, c], place[0], place[1]) for c in range(2)) for m in range(modes)
            ]

        def visit(index, carry):
            ids = [index * group + k for k in range(group)]
            turns = list(enumerate(ids))
            places = [start(w) for w in ids]
            crops, waves = {}, {}
            for k, w in turns:
                for s in forward:
                    crops[k, s] = crop(s, places[k])
                for s in backward:
                    if s not in forward:
                        crops[k, s] = tuple(r[f"crop{s}"][w, c] for c in range(2))
                        waves[k, s] = entry(w, s, places[k])
                for s in forward[:1]:
                    waves[k, s] = entry(w, s, places[k])
                if not backward:
                    for s in forward:
                        for c in range(2):
                            r[f"crop{s}"][w, c] = crops[k, s][c]
            for s in forward:
                exits = [[times(crops[k, s], wave) for wave in waves[k, s]] for k, w in turns]
                if self.far and s == forward[-1]:
                    break
                for k, w in turns:
                    waves[k, s + 1] = both_sides(exits[k], step, step_conj)
                    if not backward:
                        store(r[f"psi{s + 1}"], w, waves[k, s + 1])
            if self.far:
                exits = [both_sides(out, transform, transform_conj) for out in exits]
                for k, w in turns:
                    intensity = sum(re * re + im * im for re, im in exits[k])
                    scale = 1.0 - r["amplitude"][pl.ds(w * side, side)] * lax.rsqrt(intensity + INTENSITY_SHIFT)
                    exits[k] = [(re * scale, im * scale) for re, im in exits[k]]
                exits = [both_sides(out, transform_conj, transform) for out in exits]
            elif backward:
                exits = [load(r[f"exit{backward[0] + 1}"], w) for w in ids]
            for i, s in enumerate(backward):
                if not (self.far and i == 0):
                    exits = [both_sides(out, step_conj, step) for out in exits]
                for k, w in turns:
                    terms = [conj_times(wave, out) for wave, out in zip(waves[k, s], exits[k])]
                    keep(w, s - backward[-1], places[k], [sum(term[c] for term in terms) for c in range(2)])
                    exits[k] = [conj_times(crops[k, s], out) for out in exits[k]]
            if self.carry:
                for k, (row, lane, *_) in enumerate(places):
                    for m in range(modes):
                        for c in range(2):
                            back = turn(exits[k][m][c], (side - row) % side, (side - lane) % side)
                            r["part"][pl.ds((2 * m + c) * side, side)] += back
            elif backward:
                for k, w in turns:
                    store(r[f"exit{backward[-1]}"], w, exits[k])
            return carry

        lax.fori_loop(0, self.windows // group, visit, 0)


def give_kernel(windows, count, col_ref, *refs):
    pieces, base, out_ref = refs[:count], refs[count:-1], refs[-1]
    planes, rows, cols = out_ref.shape
    blocks = cols // LANES
    lanes = lax.broadcasted_iota(jnp.int32, (1, 1, LANES), 2)
    out_ref[...] = base[0][...] if base else jnp.zeros(out_ref.shape, jnp.float32)
    for k, piece in enumerate(pieces):
        for w in range(windows):
            col = col_ref[k, w]
            block, lane = col // LANES, col % LANES
            after = jnp.where(block + 1 == blocks, 0, block + 1)
            near, far = (pl.ds(pl.multiple_of(b * LANES, LANES), LANES) for b in (block, after))
            value = piece[pl.ds(w * planes * rows, planes * rows)].reshape(planes, rows, LANES)
            wraps = lanes < lane
            out_ref[:, :, near] += jnp.where(wraps, 0.0, value)
            out_ref[:, :, far] += jnp.where(wraps, value, 0.0)


def give(windows, columns, pieces, shape, base=()):
    smem, vmem = (pl.BlockSpec(memory_space=space) for space in (pltpu.SMEM, pltpu.VMEM))
    return pl.pallas_call(
        functools.partial(give_kernel, windows, len(pieces)),
        out_shape=jax.ShapeDtypeStruct(shape, jnp.float32),
        in_specs=[smem] + [vmem] * (len(pieces) + len(base)),
        out_specs=vmem,
        compiler_params=pltpu.CompilerParams(vmem_limit_bytes=VMEM_BYTES),
    )(jnp.stack(columns), *pieces, *base)


def fetch(*arrays):
    def kernel(*refs):
        count = len(arrays)
        sources, targets, done = refs[:count], refs[count : 2 * count], refs[-1]
        copies = [pltpu.make_async_copy(*refs, done.at[i]) for i, refs in enumerate(zip(sources, targets))]
        for copy in copies:
            copy.start()
        for copy in copies:
            copy.wait()

    anywhere, vmem = pl.BlockSpec(memory_space=pltpu.HBM), pl.BlockSpec(memory_space=pltpu.VMEM)
    return pl.pallas_call(
        kernel,
        out_shape=[jax.ShapeDtypeStruct(x.shape, x.dtype) for x in arrays],
        in_specs=[anywhere] * len(arrays),
        out_specs=[vmem] * len(arrays),
        scratch_shapes=[pltpu.SemaphoreType.DMA((len(arrays),))],
        compiler_params=pltpu.CompilerParams(vmem_limit_bytes=VMEM_BYTES),
    )(*arrays)


def moved_here(tile):
    return tile // 2 % 2


def swap(value, bits):
    count = lax.axis_size("tile")
    return lax.ppermute(value, "tile", [(i, i ^ bits) for i in range(count)])


def sum_over_tiles(total):
    bit = 8
    while bit < lax.axis_size("tile"):
        total = total + swap(total, bit)
        bit *= 2
    return total


def on_device(slices, probe_modes, row_offset, col_offset, amplitude):
    modes, _, side, _ = probe_modes.shape
    slice_count, _, rows_here, cols = slices.shape
    windows = row_offset.shape[0]
    count = lax.axis_size("tile")
    reach = side // rows_here
    assert side == LANES and side % rows_here == 0 and cols % LANES == 0
    assert reach == 4 and count % reach == 0 and count & (count - 1) == 0
    home = [(t + reach) % count if moved_here(t) else t for t in range(count)]
    to_edge = [(t, home[t]) if moved_here(t) else ((t + reach) % count, t) for t in range(count)]
    from_edge = [(b, a) for a, b in to_edge]
    even = lax.axis_index("tile") % 2 == 0
    sizes = (windows, modes, side, rows_here, cols)

    def send(value, pairs_there):
        return lax.ppermute(value, "tile", pairs_there)


    def return_route(even_step, odd_step):
        return [(home[t], (t + (odd_step if t % 2 else even_step)) % count) for t in range(count)]

    flat = slices.reshape(slice_count * 2 * rows_here, cols)
    to_home = list(enumerate(home))
    partner, edge, own_mate = swap(flat, 2), send(flat, to_edge), swap(flat, 1)
    fetched = fetch(flat, probe_modes, jnp.asarray(tables_of(side)))
    partner, *fetched = lax.optimization_barrier((partner, *fetched))
    carried = jnp.stack([row_offset, col_offset]).astype(jnp.float32)
    carried = jnp.pad(carried, ((0, EXTRA - 2), (0, side - windows)))
    measured = jnp.concatenate([amplitude.reshape(windows * side, side), carried])
    measured = send(measured, to_home)
    first_rows = swap(partner[:EXTRA], 1)
    edge, measured, first_rows = lax.optimization_barrier((edge, measured, first_rows))
    offsets = measured[windows * side :][:2, :windows].astype(jnp.int32)
    partner_mate, edge_mate = swap(partner, 1), swap(edge, 1)
    values = {
        "own": fetched[0],
        "probe": fetched[1],
        "tables": fetched[2],
        "offsets": offsets,
        "own_mate": own_mate,
        "partner": partner,
        "partner_mate": partner_mate,
        "edge": edge,
        "edge_mate": edge_mate,
        "amplitude": measured,
        "first_rows": first_rows,
    }
    chunk = list(range(slice_count))
    result = Stage(chunk, True, chunk[::-1], sizes)(values)

    part = result["part"] + swap(result["part"], 2)
    lower, upper = part[: modes * side], part[modes * side :]
    total = jnp.where(even, lower, upper) + swap(jnp.where(even, upper, lower), 1)
    pieces = [result[f"grad{j}"] for j in range(reach + 1)]
    total = total + swap(total, 4)
    outer = send(pieces[4], return_route(1, 3))
    early = [pieces[0], send(pieces[1], from_edge), outer, send(pieces[3], return_route(3, 1))]
    late = [send(pieces[2], return_route(2, 2))]
    total, *early = lax.optimization_barrier((total, *early))

    def columns_of(piece):
        return piece[-EXTRA:][:windows, 0].astype(jnp.int32)

    shape = (2 * slice_count, rows_here, cols)
    columns = [offsets[1]] + [columns_of(piece) for piece in early[1:]]
    own_grad = give(windows, columns, early, shape)
    total = sum_over_tiles(total)
    rest = swap(total, 1)
    total, rest, own_grad, *late = lax.optimization_barrier((total, rest, own_grad, *late))
    own_grad = give(windows, [columns_of(piece) for piece in late], late, shape, [own_grad])
    own_grad = own_grad.reshape(slices.shape)
    probe_grad = jnp.where(even, jnp.concatenate([total, rest]), jnp.concatenate([rest, total]))
    return own_grad, probe_grad.reshape(probe_modes.shape)


def solution(mesh):
    placed = (
        P(None, None, ("scan", "tile"), None),
        P("scan", None, None, None),
        P(("scan", "tile")),
        P(("scan", "tile")),
        P(("scan", "tile"), None, None),
    )
    return jax.shard_map(
        on_device,
        mesh=mesh,
        in_specs=placed,
        out_specs=(P(None, None, ("scan", "tile"), None), P("scan", None, None, None)),
        check_vma=False,
    )
```

```python
import functools
import math

import numpy as np
import ml_dtypes
import jax
import jax.numpy as jnp
from jax import lax
from jax.experimental import pallas as pl
from jax.experimental.pallas import tpu as pltpu
from jax.sharding import PartitionSpec as P

INTENSITY_SHIFT = 0.5
FRESNEL = 0.75
LANES = 128
VMEM_BYTES = 20 * 1024 * 1024
EXTRA = 8


def pairs(value):
    first = value.astype(ml_dtypes.bfloat16)
    second = (value - first.astype(np.float64)).astype(ml_dtypes.bfloat16)
    return np.stack([first, second])


def real_form(matrix):
    return np.block([[matrix.real, matrix.imag], [-matrix.imag, matrix.real]])


def tables_of(window_side):
    steps = np.arange(window_side)
    angles = -2.0 * math.pi / window_side * (steps[:, None] * steps[None, :] % window_side)
    transform = np.exp(1j * angles) / math.sqrt(window_side)
    freqs = (steps + window_side // 2) % window_side - window_side // 2
    phase = np.exp(-1j * math.pi * FRESNEL * freqs**2 / (window_side / 2.0) ** 2)
    step = transform.conj() @ (phase[:, None] * transform)
    forms = [real_form(m) for m in (step, step.conj(), transform, transform.conj())]
    return np.stack([pairs(form) for form in forms])


def halves(value):
    first = value.astype(jnp.bfloat16)
    return first, (value - first.astype(jnp.float32)).astype(jnp.bfloat16)


def product(left, right):
    return jnp.dot(left, right, preferred_element_type=jnp.float32)


def right_apply(field, table):
    first, second = halves(field)
    return product(first, table[0]) + (product(second, table[0]) + product(first, table[1]))


def left_apply(table, field):
    first, second = halves(field)
    return product(table[0], first) + (product(table[0], second) + product(table[1], first))


def both_sides(waves, right_table, left_table):
    side = waves[0][0].shape[0]
    rows = jnp.concatenate([jnp.concatenate(wave, axis=1) for wave in waves], axis=0)
    half = right_apply(rows, right_table)
    count = len(waves)
    parts = [
        jnp.concatenate(
            [half[m * side : (m + 1) * side, c * side : (c + 1) * side] for m in range(count)], axis=1
        )
        for c in range(2)
    ]
    full = left_apply(left_table, jnp.concatenate(parts, axis=0))
    return [
        tuple(full[c * side : (c + 1) * side, m * side : (m + 1) * side] for c in range(2))
        for m in range(count)
    ]


def times(a, b):
    return (a[0] * b[0] - a[1] * b[1], a[0] * b[1] + a[1] * b[0])


def conj_times(a, b):
    return (a[0] * b[0] + a[1] * b[1], a[0] * b[1] - a[1] * b[0])


class Stage:
    def __init__(self, forward, far, backward, sizes):
        self.forward, self.far, self.backward = forward, far, backward
        self.windows, self.modes, self.side, self.rows_here, self.cols = sizes
        self.reach = self.side // self.rows_here
        self.carry = 0 in backward
        self.grad_rows = self.windows * len(backward) * 2 * self.rows_here
        self.group = math.gcd(self.windows, 4)
        loaded = set(backward) - set(forward)
        waves = loaded | set(forward[:1])
        vmem = ["tables"]
        vmem += ["probe"] if 0 in waves else []
        vmem += ["amplitude"] if far else []
        vmem += [f"psi{s}" for s in sorted(waves) if s > 0] + [f"crop{s}" for s in sorted(loaded)]
        vmem += [] if far else [f"exit{s + 1}" for s in backward[:1]]
        if forward:
            vmem += ["own", "own_mate", "partner", "partner_mate", "edge", "edge_mate", "first_rows"]
        self.vmem_in = vmem
        outs = [f"grad{j}" for j in range(self.reach + 1)] if backward else []
        if not backward:
            outs += [f"psi{s + 1}" for s in forward] + [f"crop{s}" for s in forward]
        else:
            outs.append("part" if self.carry else f"exit{backward[-1]}")
        self.vmem_out = outs
        if backward:
            outs += [f"grad{j}" for j in range(self.reach + 1)]

    def out_shape(self, name):
        side = self.side
        if name.startswith("grad"):
            shape = (self.grad_rows + (EXTRA if self.carry else 0), side)
        elif name == "part":
            shape = (2 * self.modes * side, side)
        elif name.startswith("crop"):
            shape = (self.windows, 2, side, side)
        else:
            shape = (self.windows, self.modes, 2, side, side)
        return jax.ShapeDtypeStruct(shape, jnp.float32)

    def __call__(self, values):
        inputs = ["offsets"] + self.vmem_in
        outputs = self.vmem_out
        args = [values[name] for name in inputs]
        shapes = [self.out_shape(name) for name in outputs]
        smem, vmem = (pl.BlockSpec(memory_space=space) for space in (pltpu.SMEM, pltpu.VMEM))
        outs = pl.pallas_call(
            self.kernel,
            out_shape=shapes,
            in_specs=[smem] + [vmem] * len(self.vmem_in),
            out_specs=[vmem] * len(self.vmem_out),
            cost_estimate=pl.CostEstimate(flops=0, bytes_accessed=0, transcendentals=0),
            compiler_params=pltpu.CompilerParams(vmem_limit_bytes=VMEM_BYTES),
        )(*args)
        return dict(zip(outputs, outs))

    def kernel(self, *refs):
        names = ["offsets"] + self.vmem_in + self.vmem_out
        r = dict(zip(names, refs))
        side, rows_here, modes, group = self.side, self.rows_here, self.modes, self.group
        forward, backward = self.forward, self.backward
        step, step_conj, transform, transform_conj = (
            (r["tables"][i, 0], r["tables"][i, 1]) for i in range(4)
        )
        me = lax.axis_index("tile")
        parity, moved = me % 2, moved_here(me)
        blocks = self.cols // LANES

        if self.carry:
            index = lax.broadcasted_iota(jnp.int32, (EXTRA, side), 0)
            carried = jnp.zeros((EXTRA, side), jnp.int32)
            for w in range(self.windows):
                carried = jnp.where(index == w, r["offsets"][1, w], carried)
            for j in range(1, self.reach + 1):
                r[f"grad{j}"][pl.ds(self.grad_rows, EXTRA)] = carried.astype(jnp.float32)
            r["part"][...] = jnp.zeros(r["part"].shape, jnp.float32)
        def start(w):
            row, col = r["offsets"][0, w], r["offsets"][1, w]
            block = col // LANES
            after = jnp.where(block + 1 == blocks, 0, block + 1)
            near, far = (pl.ds(pl.multiple_of(b * LANES, LANES), LANES) for b in (block, after))
            lane = col % LANES
            below = lax.broadcasted_iota(jnp.int32, (rows_here, side), 0) >= row
            here = jnp.where(below, 1, 0) != moved
            wraps = lax.broadcasted_iota(jnp.int32, (rows_here, side), 1) < lane
            return row, lane, near, far, here, wraps

        def crop(s, place):
            _, _, near, far, here, wraps = place

            def columns(name, c):
                tile = r[name].at[pl.ds((2 * s + c) * rows_here, rows_here)]
                return jnp.where(wraps, tile[:, far], tile[:, near])

            def plane(c):
                first = jnp.where(here, columns("own", c), columns("edge", c))
                outer = jnp.where(parity == moved, columns("own_mate", c), columns("edge_mate", c))
                inner = columns("partner_mate", c)
                pair = [jnp.where(parity == 0, a, b) for a, b in ((outer, inner), (inner, outer))]
                return jnp.concatenate([first, pair[0], columns("partner", c), pair[1]], axis=0)

            return (plane(0), plane(1))

        def keep(w, i, place, grad):
            here = place[4]
            for c in range(2):
                at = rows_at(((w * len(backward) + i) * 2 + c), rows_here)
                edge = grad[c][:rows_here]
                r["grad0"][at] = jnp.where(here, edge, 0.0)
                r["grad1"][at] = jnp.where(here, 0.0, edge)
                for j in range(1, self.reach):
                    r[f"grad{j + 1}"][at] = grad[c][j * rows_here : (j + 1) * rows_here]

        def turn(value, row, lane):
            return pltpu.roll(pltpu.roll(value, row, 0), lane, 1)

        def load(ref, w):
            return [tuple(ref[w, m, c] for c in range(2)) for m in range(modes)]

        def store(ref, w, waves):
            for m in range(modes):
                for c in range(2):
                    ref[w, m, c] = waves[m][c]

        def entry(w, s, place):
            if s > 0:
                return load(r[f"psi{s}"], w)
            return [
                tuple(turn(r["probe"][m, c], place[0], place[1]) for c in range(2)) for m in range(modes)
            ]

        def visit(index, carry):
            ids = [index * group + k for k in range(group)]
            turns = list(enumerate(ids))
            places = [start(w) for w in ids]
            crops, waves = {}, {}
            for k, w in turns:
                for s in forward:
                    crops[k, s] = crop(s, places[k])
                for s in backward:
                    if s not in forward:
                        crops[k, s] = tuple(r[f"crop{s}"][w, c] for c in range(2))
                        waves[k, s] = entry(w, s, places[k])
                for s in forward[:1]:
                    waves[k, s] = entry(w, s, places[k])
                if not backward:
                    for s in forward:
                        for c in range(2):
                            r[f"crop{s}"][w, c] = crops[k, s][c]
            for s in forward:
                exits = [[times(crops[k, s], wave) for wave in waves[k, s]] for k, w in turns]
                if self.far and s == forward[-1]:
                    break
                for k, w in turns:
                    waves[k, s + 1] = both_sides(exits[k], step, step_conj)
                    if not backward:
                        store(r[f"psi{s + 1}"], w, waves[k, s + 1])
            if self.far:
                exits = [both_sides(out, transform, transform_conj) for out in exits]
                for k, w in turns:
                    intensity = sum(re * re + im * im for re, im in exits[k])
                    scale = 1.0 - r["amplitude"][rows_at(w, side)] * lax.rsqrt(intensity + INTENSITY_SHIFT)
                    exits[k] = [(re * scale, im * scale) for re, im in exits[k]]
                exits = [both_sides(out, transform_conj, transform) for out in exits]
            elif backward:
                exits = [load(r[f"exit{backward[0] + 1}"], w) for w in ids]
            for i, s in enumerate(backward):
                if not (self.far and i == 0):
                    exits = [both_sides(out, step_conj, step) for out in exits]
                for k, w in turns:
                    terms = [conj_times(wave, out) for wave, out in zip(waves[k, s], exits[k])]
                    keep(w, s - backward[-1], places[k], [sum(term[c] for term in terms) for c in range(2)])
                    exits[k] = [conj_times(crops[k, s], out) for out in exits[k]]
            if self.carry:
                for k, (row, lane, *_) in enumerate(places):
                    for m in range(modes):
                        for c in range(2):
                            back = turn(exits[k][m][c], (side - row) % side, (side - lane) % side)
                            r["part"][pl.ds((2 * m + c) * side, side)] += back
            elif backward:
                for k, w in turns:
                    store(r[f"exit{backward[-1]}"], w, exits[k])
            return carry

        if self.windows == group:
            visit(0, 0)
        else:
            lax.fori_loop(0, self.windows // group, visit, 0)


def give_kernel(windows, count, col_ref, *refs):
    pieces, base, out_ref = refs[:count], refs[count:-1], refs[-1]
    planes, rows, cols = out_ref.shape
    blocks = cols // LANES
    lanes = lax.broadcasted_iota(jnp.int32, (1, 1, LANES), 2)
    out_ref[...] = base[0][...] if base else jnp.zeros(out_ref.shape, jnp.float32)
    for k, piece in enumerate(pieces):
        for w in range(windows):
            col = col_ref[k, w]
            block, lane = col // LANES, col % LANES
            after = jnp.where(block + 1 == blocks, 0, block + 1)
            near, far = (pl.ds(pl.multiple_of(b * LANES, LANES), LANES) for b in (block, after))
            value = piece[pl.ds(w * planes * rows, planes * rows)].reshape(planes, rows, LANES)
            wraps = lanes < lane
            out_ref[:, :, near] += jnp.where(wraps, 0.0, value)
            out_ref[:, :, far] += jnp.where(wraps, value, 0.0)


def give(windows, columns, pieces, shape, base=()):
    smem, vmem = (pl.BlockSpec(memory_space=space) for space in (pltpu.SMEM, pltpu.VMEM))
    return pl.pallas_call(
        functools.partial(give_kernel, windows, len(pieces)),
        out_shape=jax.ShapeDtypeStruct(shape, jnp.float32),
        in_specs=[smem] + [vmem] * (len(pieces) + len(base)),
        out_specs=vmem,
        compiler_params=pltpu.CompilerParams(vmem_limit_bytes=VMEM_BYTES),
    )(jnp.stack(columns), *pieces, *base)


def fetch(*arrays):
    def kernel(*refs):
        count = len(arrays)
        sources, targets, done = refs[:count], refs[count : 2 * count], refs[-1]
        copies = [pltpu.make_async_copy(*refs, done.at[i]) for i, refs in enumerate(zip(sources, targets))]
        for copy in copies:
            copy.start()
        for copy in copies:
            copy.wait()

    anywhere, vmem = pl.BlockSpec(memory_space=pltpu.HBM), pl.BlockSpec(memory_space=pltpu.VMEM)
    return pl.pallas_call(
        kernel,
        out_shape=[jax.ShapeDtypeStruct(x.shape, x.dtype) for x in arrays],
        in_specs=[anywhere] * len(arrays),
        out_specs=[vmem] * len(arrays),
        scratch_shapes=[pltpu.SemaphoreType.DMA((len(arrays),))],
        compiler_params=pltpu.CompilerParams(vmem_limit_bytes=VMEM_BYTES),
    )(*arrays)


def rows_at(block, size):
    first = block * size
    return pl.ds(first if isinstance(first, int) else pl.multiple_of(first, size), size)


def moved_here(tile):
    return tile // 2 % 2


def swap(value, bits):
    count = lax.axis_size("tile")
    return lax.ppermute(value, "tile", [(i, i ^ bits) for i in range(count)])


def sum_over_tiles(total):
    bit = 8
    while bit < lax.axis_size("tile"):
        total = total + swap(total, bit)
        bit *= 2
    return total


def on_device(slices, probe_modes, row_offset, col_offset, amplitude):
    modes, _, side, _ = probe_modes.shape
    slice_count, _, rows_here, cols = slices.shape
    windows = row_offset.shape[0]
    count = lax.axis_size("tile")
    reach = side // rows_here
    assert side == LANES and side % rows_here == 0 and cols % LANES == 0
    assert reach == 4 and count % reach == 0 and count & (count - 1) == 0
    home = [(t + reach) % count if moved_here(t) else t for t in range(count)]
    to_edge = [(t, home[t]) if moved_here(t) else ((t + reach) % count, t) for t in range(count)]
    from_edge = [(b, a) for a, b in to_edge]
    even = lax.axis_index("tile") % 2 == 0
    sizes = (windows, modes, side, rows_here, cols)

    def send(value, pairs_there):
        return lax.ppermute(value, "tile", pairs_there)


    def return_route(step):
        return [(home[t], (t + step) % count) for t in range(count)]

    flat = slices.reshape(slice_count * 2 * rows_here, cols)
    to_home = list(enumerate(home))
    partner, edge, own_mate = swap(flat, 2), send(flat, to_edge), swap(flat, 1)
    fetched = fetch(flat, probe_modes, jnp.asarray(tables_of(side)))
    partner, *fetched = lax.optimization_barrier((partner, *fetched))
    carried = jnp.stack([row_offset, col_offset]).astype(jnp.float32)
    carried = jnp.pad(carried, ((0, EXTRA - 2), (0, side - windows)))
    measured = jnp.concatenate([amplitude.reshape(windows * side, side), carried])
    measured = send(measured, to_home)
    first_rows = swap(partner[:EXTRA], 1)
    edge, measured, first_rows = lax.optimization_barrier((edge, measured, first_rows))
    offsets = measured[windows * side :][:2, :windows].astype(jnp.int32)
    partner_mate, edge_mate = swap(partner, 1), swap(edge, 1)
    values = {
        "own": fetched[0],
        "probe": fetched[1],
        "tables": fetched[2],
        "offsets": offsets,
        "own_mate": own_mate,
        "partner": partner,
        "partner_mate": partner_mate,
        "edge": edge,
        "edge_mate": edge_mate,
        "amplitude": measured,
        "first_rows": first_rows,
    }
    chunk = list(range(slice_count))
    result = Stage(chunk, True, chunk[::-1], sizes)(values)

    part = result["part"] + swap(result["part"], 2)
    lower, upper = part[: modes * side], part[modes * side :]
    total = jnp.where(even, lower, upper) + swap(jnp.where(even, upper, lower), 1)
    pieces = [result[f"grad{j}"] for j in range(reach + 1)]
    total = total + swap(total, 4)
    middle = reach // 2 + 1
    early = [pieces[0], send(pieces[1], from_edge)]
    early += [send(pieces[j], return_route(j - 1)) for j in range(2, reach + 1) if j != middle]
    late = send(pieces[middle], return_route(middle - 1))
    total, *early = lax.optimization_barrier((total, *early))

    def columns_of(piece):
        return piece[-EXTRA:][:windows, 0].astype(jnp.int32)

    shape = (2 * slice_count, rows_here, cols)
    columns = [offsets[1]] + [columns_of(piece) for piece in early[1:]]
    own_grad = give(windows, columns, early, shape)
    total = sum_over_tiles(total)
    total, own_grad, late = lax.optimization_barrier((total, own_grad, late))
    own_grad = give(windows, [columns_of(late)], [late], shape, [own_grad]).reshape(slices.shape)
    rest = swap(total, 1)
    probe_grad = jnp.where(even, jnp.concatenate([total, rest]), jnp.concatenate([rest, total]))
    return own_grad, probe_grad.reshape(probe_modes.shape)


def solution(mesh):
    placed = (
        P(None, None, ("scan", "tile"), None),
        P("scan", None, None, None),
        P(("scan", "tile")),
        P(("scan", "tile")),
        P(("scan", "tile"), None, None),
    )
    return jax.shard_map(
        on_device,
        mesh=mesh,
        in_specs=placed,
        out_specs=(P(None, None, ("scan", "tile"), None), P("scan", None, None, None)),
        check_vma=False,
    )
```

```python
import functools
import math

import numpy as np
import ml_dtypes
import jax
import jax.numpy as jnp
from jax import lax
from jax.experimental import pallas as pl
from jax.experimental.pallas import tpu as pltpu
from jax.sharding import PartitionSpec as P

INTENSITY_SHIFT = 0.5
FRESNEL = 0.75
LANES = 128
VMEM_BYTES = 20 * 1024 * 1024
EXTRA = 8


def pairs(value):
    first = value.astype(ml_dtypes.bfloat16)
    second = (value - first.astype(np.float64)).astype(ml_dtypes.bfloat16)
    return np.stack([first, second])


def real_form(matrix):
    return np.block([[matrix.real, matrix.imag], [-matrix.imag, matrix.real]])


def tables_of(window_side):
    steps = np.arange(window_side)
    angles = -2.0 * math.pi / window_side * (steps[:, None] * steps[None, :] % window_side)
    transform = np.exp(1j * angles) / math.sqrt(window_side)
    freqs = (steps + window_side // 2) % window_side - window_side // 2
    phase = np.exp(-1j * math.pi * FRESNEL * freqs**2 / (window_side / 2.0) ** 2)
    step = transform.conj() @ (phase[:, None] * transform)
    forms = [real_form(m) for m in (step, step.conj(), transform, transform.conj())]
    return np.stack([pairs(form) for form in forms])


def halves(value):
    first = value.astype(jnp.bfloat16)
    return first, (value - first.astype(jnp.float32)).astype(jnp.bfloat16)


def product(left, right):
    return jnp.dot(left, right, preferred_element_type=jnp.float32)


def right_apply(field, table):
    first, second = halves(field)
    return product(first, table[0]) + (product(second, table[0]) + product(first, table[1]))


def left_apply(table, field):
    first, second = halves(field)
    return product(table[0], first) + (product(table[0], second) + product(table[1], first))


def both_sides(waves, right_table, left_table):
    side = waves[0][0].shape[0]
    rows = jnp.concatenate([jnp.concatenate(wave, axis=1) for wave in waves], axis=0)
    half = right_apply(rows, right_table)
    count = len(waves)
    parts = [
        jnp.concatenate(
            [half[m * side : (m + 1) * side, c * side : (c + 1) * side] for m in range(count)], axis=1
        )
        for c in range(2)
    ]
    full = left_apply(left_table, jnp.concatenate(parts, axis=0))
    return [
        tuple(full[c * side : (c + 1) * side, m * side : (m + 1) * side] for c in range(2))
        for m in range(count)
    ]


def times(a, b):
    return (a[0] * b[0] - a[1] * b[1], a[0] * b[1] + a[1] * b[0])


def conj_times(a, b):
    return (a[0] * b[0] + a[1] * b[1], a[0] * b[1] - a[1] * b[0])


class Stage:
    def __init__(self, forward, far, backward, sizes):
        self.forward, self.far, self.backward = forward, far, backward
        self.windows, self.modes, self.side, self.rows_here, self.cols = sizes
        self.reach = self.side // self.rows_here
        self.carry = 0 in backward
        self.grad_rows = self.windows * len(backward) * 2 * self.rows_here
        self.group = math.gcd(self.windows, 4)
        loaded = set(backward) - set(forward)
        waves = loaded | set(forward[:1])
        vmem = ["tables"]
        vmem += ["probe"] if 0 in waves else []
        vmem += ["amplitude"] if far else []
        vmem += [f"psi{s}" for s in sorted(waves) if s > 0] + [f"crop{s}" for s in sorted(loaded)]
        vmem += [] if far else [f"exit{s + 1}" for s in backward[:1]]
        if forward:
            vmem += ["own", "own_mate", "partner", "partner_mate", "edge", "edge_mate"]
        self.vmem_in = vmem
        outs = [f"grad{j}" for j in range(self.reach + 1)] if backward else []
        if not backward:
            outs += [f"psi{s + 1}" for s in forward] + [f"crop{s}" for s in forward]
        else:
            outs.append("part" if self.carry else f"exit{backward[-1]}")
        self.vmem_out = outs
        if backward:
            outs += [f"grad{j}" for j in range(self.reach + 1)]

    def out_shape(self, name):
        side = self.side
        if name.startswith("grad"):
            shape = (self.grad_rows + (EXTRA if self.carry else 0), side)
        elif name == "part":
            shape = (2 * self.modes * side, side)
        elif name.startswith("crop"):
            shape = (self.windows, 2, side, side)
        else:
            shape = (self.windows, self.modes, 2, side, side)
        return jax.ShapeDtypeStruct(shape, jnp.float32)

    def __call__(self, values):
        inputs = ["offsets"] + self.vmem_in
        outputs = self.vmem_out
        args = [values[name] for name in inputs]
        shapes = [self.out_shape(name) for name in outputs]
        smem, vmem = (pl.BlockSpec(memory_space=space) for space in (pltpu.SMEM, pltpu.VMEM))
        outs = pl.pallas_call(
            self.kernel,
            out_shape=shapes,
            in_specs=[smem] + [vmem] * len(self.vmem_in),
            out_specs=[vmem] * len(self.vmem_out),
            cost_estimate=pl.CostEstimate(flops=0, bytes_accessed=0, transcendentals=0),
            compiler_params=pltpu.CompilerParams(vmem_limit_bytes=VMEM_BYTES),
        )(*args)
        return dict(zip(outputs, outs))

    def kernel(self, *refs):
        names = ["offsets"] + self.vmem_in + self.vmem_out
        r = dict(zip(names, refs))
        side, rows_here, modes, group = self.side, self.rows_here, self.modes, self.group
        forward, backward = self.forward, self.backward
        step, step_conj, transform, transform_conj = (
            (r["tables"][i, 0], r["tables"][i, 1]) for i in range(4)
        )
        me = lax.axis_index("tile")
        parity, moved = me % 2, moved_here(me)
        blocks = self.cols // LANES

        if self.carry:
            index = lax.broadcasted_iota(jnp.int32, (EXTRA, side), 0)
            carried = jnp.zeros((EXTRA, side), jnp.int32)
            for w in range(self.windows):
                carried = jnp.where(index == w, r["offsets"][1, w], carried)
            for j in range(1, self.reach + 1):
                r[f"grad{j}"][pl.ds(self.grad_rows, EXTRA)] = carried.astype(jnp.float32)
            r["part"][...] = jnp.zeros(r["part"].shape, jnp.float32)
        def start(w):
            row, col = r["offsets"][0, w], r["offsets"][1, w]
            block = col // LANES
            after = jnp.where(block + 1 == blocks, 0, block + 1)
            near, far = (pl.ds(pl.multiple_of(b * LANES, LANES), LANES) for b in (block, after))
            lane = col % LANES
            below = lax.broadcasted_iota(jnp.int32, (rows_here, side), 0) >= row
            here = jnp.where(below, 1, 0) != moved
            wraps = lax.broadcasted_iota(jnp.int32, (rows_here, side), 1) < lane
            return row, lane, near, far, here, wraps

        def crop(s, place):
            _, _, near, far, here, wraps = place

            def columns(name, c):
                tile = r[name].at[pl.ds((2 * s + c) * rows_here, rows_here)]
                return jnp.where(wraps, tile[:, far], tile[:, near])

            def plane(c):
                first = jnp.where(here, columns("own", c), columns("edge", c))
                outer = jnp.where(parity == moved, columns("own_mate", c), columns("edge_mate", c))
                inner = columns("partner_mate", c)
                pair = [jnp.where(parity == 0, a, b) for a, b in ((outer, inner), (inner, outer))]
                return jnp.concatenate([first, pair[0], columns("partner", c), pair[1]], axis=0)

            return (plane(0), plane(1))

        def keep(w, i, place, grad):
            here = place[4]
            for c in range(2):
                at = rows_at(((w * len(backward) + i) * 2 + c), rows_here)
                edge = grad[c][:rows_here]
                r["grad0"][at] = jnp.where(here, edge, 0.0)
                r["grad1"][at] = jnp.where(here, 0.0, edge)
                for j in range(1, self.reach):
                    r[f"grad{j + 1}"][at] = grad[c][j * rows_here : (j + 1) * rows_here]

        def turn(value, row, lane):
            return pltpu.roll(pltpu.roll(value, row, 0), lane, 1)

        def load(ref, w):
            return [tuple(ref[w, m, c] for c in range(2)) for m in range(modes)]

        def store(ref, w, waves):
            for m in range(modes):
                for c in range(2):
                    ref[w, m, c] = waves[m][c]

        def entry(w, s, place):
            if s > 0:
                return load(r[f"psi{s}"], w)
            return [
                tuple(turn(r["probe"][m, c], place[0], place[1]) for c in range(2)) for m in range(modes)
            ]

        def visit(index, carry):
            ids = [index * group + k for k in range(group)]
            turns = list(enumerate(ids))
            places = [start(w) for w in ids]
            crops, waves = {}, {}
            for k, w in turns:
                for s in forward:
                    crops[k, s] = crop(s, places[k])
                for s in backward:
                    if s not in forward:
                        crops[k, s] = tuple(r[f"crop{s}"][w, c] for c in range(2))
                        waves[k, s] = entry(w, s, places[k])
                for s in forward[:1]:
                    waves[k, s] = entry(w, s, places[k])
                if not backward:
                    for s in forward:
                        for c in range(2):
                            r[f"crop{s}"][w, c] = crops[k, s][c]
            for s in forward:
                exits = [[times(crops[k, s], wave) for wave in waves[k, s]] for k, w in turns]
                if self.far and s == forward[-1]:
                    break
                for k, w in turns:
                    waves[k, s + 1] = both_sides(exits[k], step, step_conj)
                    if not backward:
                        store(r[f"psi{s + 1}"], w, waves[k, s + 1])
            if self.far:
                exits = [both_sides(out, transform, transform_conj) for out in exits]
                for k, w in turns:
                    intensity = sum(re * re + im * im for re, im in exits[k])
                    scale = 1.0 - r["amplitude"][rows_at(w, side)] * lax.rsqrt(intensity + INTENSITY_SHIFT)
                    exits[k] = [(re * scale, im * scale) for re, im in exits[k]]
                exits = [both_sides(out, transform_conj, transform) for out in exits]
            elif backward:
                exits = [load(r[f"exit{backward[0] + 1}"], w) for w in ids]
            for i, s in enumerate(backward):
                if not (self.far and i == 0):
                    exits = [both_sides(out, step_conj, step) for out in exits]
                for k, w in turns:
                    terms = [conj_times(wave, out) for wave, out in zip(waves[k, s], exits[k])]
                    keep(w, s - backward[-1], places[k], [sum(term[c] for term in terms) for c in range(2)])
                    exits[k] = [conj_times(crops[k, s], out) for out in exits[k]]
            if self.carry:
                for k, (row, lane, *_) in enumerate(places):
                    for m in range(modes):
                        for c in range(2):
                            back = turn(exits[k][m][c], (side - row) % side, (side - lane) % side)
                            r["part"][pl.ds((2 * m + c) * side, side)] += back
            elif backward:
                for k, w in turns:
                    store(r[f"exit{backward[-1]}"], w, exits[k])
            return carry

        if self.windows == group:
            visit(0, 0)
        else:
            lax.fori_loop(0, self.windows // group, visit, 0)


def give_kernel(windows, count, col_ref, *refs):
    pieces, base, out_ref = refs[:count], refs[count:-1], refs[-1]
    planes, rows, cols = out_ref.shape
    blocks = cols // LANES
    lanes = lax.broadcasted_iota(jnp.int32, (1, 1, LANES), 2)
    out_ref[...] = base[0][...] if base else jnp.zeros(out_ref.shape, jnp.float32)
    for k, piece in enumerate(pieces):
        for w in range(windows):
            col = col_ref[k, w]
            block, lane = col // LANES, col % LANES
            after = jnp.where(block + 1 == blocks, 0, block + 1)
            near, far = (pl.ds(pl.multiple_of(b * LANES, LANES), LANES) for b in (block, after))
            value = piece[pl.ds(w * planes * rows, planes * rows)].reshape(planes, rows, LANES)
            wraps = lanes < lane
            out_ref[:, :, near] += jnp.where(wraps, 0.0, value)
            out_ref[:, :, far] += jnp.where(wraps, value, 0.0)


def give(windows, columns, pieces, shape, base=()):
    smem, vmem = (pl.BlockSpec(memory_space=space) for space in (pltpu.SMEM, pltpu.VMEM))
    return pl.pallas_call(
        functools.partial(give_kernel, windows, len(pieces)),
        out_shape=jax.ShapeDtypeStruct(shape, jnp.float32),
        in_specs=[smem] + [vmem] * (len(pieces) + len(base)),
        out_specs=vmem,
        compiler_params=pltpu.CompilerParams(vmem_limit_bytes=VMEM_BYTES),
    )(jnp.stack(columns), *pieces, *base)


def fetch(*arrays):
    def kernel(*refs):
        count = len(arrays)
        sources, targets, done = refs[:count], refs[count : 2 * count], refs[-1]
        copies = [pltpu.make_async_copy(*refs, done.at[i]) for i, refs in enumerate(zip(sources, targets))]
        for copy in copies:
            copy.start()
        for copy in copies:
            copy.wait()

    anywhere, vmem = pl.BlockSpec(memory_space=pltpu.HBM), pl.BlockSpec(memory_space=pltpu.VMEM)
    return pl.pallas_call(
        kernel,
        out_shape=[jax.ShapeDtypeStruct(x.shape, x.dtype) for x in arrays],
        in_specs=[anywhere] * len(arrays),
        out_specs=[vmem] * len(arrays),
        scratch_shapes=[pltpu.SemaphoreType.DMA((len(arrays),))],
        compiler_params=pltpu.CompilerParams(vmem_limit_bytes=VMEM_BYTES),
    )(*arrays)


def offsets_of(measured):
    def kernel(source, target):
        target[...] = source[pl.ds(source.shape[0] - EXTRA, EXTRA)].astype(jnp.int32)

    vmem = pl.BlockSpec(memory_space=pltpu.VMEM)
    return pl.pallas_call(
        kernel,
        out_shape=jax.ShapeDtypeStruct((EXTRA, measured.shape[1]), jnp.int32),
        in_specs=[vmem],
        out_specs=vmem,
        cost_estimate=pl.CostEstimate(flops=20_000_000_000, bytes_accessed=40_000_000, transcendentals=0),
        compiler_params=pltpu.CompilerParams(vmem_limit_bytes=VMEM_BYTES),
    )(measured)


def rows_at(block, size):
    first = block * size
    return pl.ds(first if isinstance(first, int) else pl.multiple_of(first, size), size)


def moved_here(tile):
    return tile // 2 % 2


def swap(value, bits):
    count = lax.axis_size("tile")
    return lax.ppermute(value, "tile", [(i, i ^ bits) for i in range(count)])


def sum_over_tiles(total):
    bit = 8
    while bit < lax.axis_size("tile"):
        total = total + swap(total, bit)
        bit *= 2
    return total


def on_device(slices, probe_modes, row_offset, col_offset, amplitude):
    modes, _, side, _ = probe_modes.shape
    slice_count, _, rows_here, cols = slices.shape
    windows = row_offset.shape[0]
    count = lax.axis_size("tile")
    reach = side // rows_here
    assert side == LANES and side % rows_here == 0 and cols % LANES == 0
    assert reach == 4 and count % reach == 0 and count & (count - 1) == 0
    home = [(t + reach) % count if moved_here(t) else t for t in range(count)]
    to_edge = [(t, home[t]) if moved_here(t) else ((t + reach) % count, t) for t in range(count)]
    from_edge = [(b, a) for a, b in to_edge]
    even = lax.axis_index("tile") % 2 == 0
    sizes = (windows, modes, side, rows_here, cols)

    def send(value, pairs_there):
        return lax.ppermute(value, "tile", pairs_there)


    def return_route(step):
        return [(home[t], (t + step) % count) for t in range(count)]

    flat = slices.reshape(slice_count * 2 * rows_here, cols)
    to_home = list(enumerate(home))
    partner, edge, own_mate = swap(flat, 2), send(flat, to_edge), swap(flat, 1)
    fetched = fetch(flat, probe_modes, jnp.asarray(tables_of(side)))
    partner, *fetched = lax.optimization_barrier((partner, *fetched))
    carried = jnp.stack([row_offset, col_offset]).astype(jnp.float32)
    carried = jnp.pad(carried, ((0, EXTRA - 2), (0, side - windows)))
    measured = jnp.concatenate([amplitude.reshape(windows * side, side), carried])
    measured = send(measured, to_home)
    offsets = offsets_of(measured)
    partner_mate, edge_mate = swap(partner, 1), swap(edge, 1)
    values = {
        "own": fetched[0],
        "probe": fetched[1],
        "tables": fetched[2],
        "offsets": offsets,
        "own_mate": own_mate,
        "partner": partner,
        "partner_mate": partner_mate,
        "edge": edge,
        "edge_mate": edge_mate,
        "amplitude": measured,
    }
    chunk = list(range(slice_count))
    result = Stage(chunk, True, chunk[::-1], sizes)(values)

    part = result["part"] + swap(result["part"], 2)
    lower, upper = part[: modes * side], part[modes * side :]
    total = jnp.where(even, lower, upper) + swap(jnp.where(even, upper, lower), 1)
    pieces = [result[f"grad{j}"] for j in range(reach + 1)]
    total = total + swap(total, 4)
    middle = reach // 2 + 1
    early = [pieces[0], send(pieces[1], from_edge)]
    early += [send(pieces[j], return_route(j - 1)) for j in range(2, reach + 1) if j != middle]
    late = send(pieces[middle], return_route(middle - 1))
    total, *early = lax.optimization_barrier((total, *early))

    def columns_of(piece):
        return piece[-EXTRA:][:windows, 0].astype(jnp.int32)

    shape = (2 * slice_count, rows_here, cols)
    columns = [offsets[1, :windows]] + [columns_of(piece) for piece in early[1:]]
    own_grad = give(windows, columns, early, shape)
    total = sum_over_tiles(total)
    total, own_grad, late = lax.optimization_barrier((total, own_grad, late))
    own_grad = give(windows, [columns_of(late)], [late], shape, [own_grad]).reshape(slices.shape)
    rest = swap(total, 1)
    probe_grad = jnp.where(even, jnp.concatenate([total, rest]), jnp.concatenate([rest, total]))
    return own_grad, probe_grad.reshape(probe_modes.shape)


def solution(mesh):
    placed = (
        P(None, None, ("scan", "tile"), None),
        P("scan", None, None, None),
        P(("scan", "tile")),
        P(("scan", "tile")),
        P(("scan", "tile"), None, None),
    )
    return jax.shard_map(
        on_device,
        mesh=mesh,
        in_specs=placed,
        out_specs=(P(None, None, ("scan", "tile"), None), P("scan", None, None, None)),
        check_vma=False,
    )
```

```python
import functools
import math

import numpy as np
import ml_dtypes
import jax
import jax.numpy as jnp
from jax import lax
from jax.experimental import pallas as pl
from jax.experimental.pallas import tpu as pltpu
from jax.sharding import PartitionSpec as P

INTENSITY_SHIFT = 0.5
FRESNEL = 0.75
LANES = 128
VMEM_BYTES = 20 * 1024 * 1024
EXTRA = 8


def pairs(value):
    first = value.astype(ml_dtypes.bfloat16)
    second = (value - first.astype(np.float64)).astype(ml_dtypes.bfloat16)
    return np.stack([first, second])


def real_form(matrix):
    return np.block([[matrix.real, matrix.imag], [-matrix.imag, matrix.real]])


def tables_of(window_side):
    steps = np.arange(window_side)
    angles = -2.0 * math.pi / window_side * (steps[:, None] * steps[None, :] % window_side)
    transform = np.exp(1j * angles) / math.sqrt(window_side)
    freqs = (steps + window_side // 2) % window_side - window_side // 2
    phase = np.exp(-1j * math.pi * FRESNEL * freqs**2 / (window_side / 2.0) ** 2)
    step = transform.conj() @ (phase[:, None] * transform)
    forms = [real_form(m) for m in (step, step.conj(), transform, transform.conj())]
    return np.stack([pairs(form) for form in forms])


def halves(value):
    first = value.astype(jnp.bfloat16)
    return first, (value - first.astype(jnp.float32)).astype(jnp.bfloat16)


def product(left, right):
    return jnp.dot(left, right, preferred_element_type=jnp.float32)


def right_apply(field, table):
    first, second = halves(field)
    return product(first, table[0]) + (product(second, table[0]) + product(first, table[1]))


def left_apply(table, field):
    first, second = halves(field)
    return product(table[0], first) + (product(table[0], second) + product(table[1], first))


def both_sides(waves, right_table, left_table):
    side = waves[0][0].shape[0]
    rows = jnp.concatenate([jnp.concatenate(wave, axis=1) for wave in waves], axis=0)
    half = right_apply(rows, right_table)
    count = len(waves)
    parts = [
        jnp.concatenate(
            [half[m * side : (m + 1) * side, c * side : (c + 1) * side] for m in range(count)], axis=1
        )
        for c in range(2)
    ]
    full = left_apply(left_table, jnp.concatenate(parts, axis=0))
    return [
        tuple(full[c * side : (c + 1) * side, m * side : (m + 1) * side] for c in range(2))
        for m in range(count)
    ]


def times(a, b):
    return (a[0] * b[0] - a[1] * b[1], a[0] * b[1] + a[1] * b[0])


def conj_times(a, b):
    return (a[0] * b[0] + a[1] * b[1], a[0] * b[1] - a[1] * b[0])


class Stage:
    def __init__(self, forward, far, backward, sizes):
        self.forward, self.far, self.backward = forward, far, backward
        self.windows, self.modes, self.side, self.rows_here, self.cols = sizes
        self.reach = self.side // self.rows_here
        self.carry = 0 in backward
        self.grad_rows = self.windows * len(backward) * 2 * self.rows_here
        self.group = math.gcd(self.windows, 4)
        loaded = set(backward) - set(forward)
        waves = loaded | set(forward[:1])
        vmem = ["tables"]
        vmem += ["probe"] if 0 in waves else []
        vmem += ["amplitude"] if far else []
        vmem += [f"psi{s}" for s in sorted(waves) if s > 0] + [f"crop{s}" for s in sorted(loaded)]
        vmem += [] if far else [f"exit{s + 1}" for s in backward[:1]]
        if forward:
            vmem += ["own", "own_mate", "partner", "partner_mate", "edge", "edge_mate"]
        self.vmem_in = vmem
        outs = [f"grad{j}" for j in range(self.reach + 1)] if backward else []
        if not backward:
            outs += [f"psi{s + 1}" for s in forward] + [f"crop{s}" for s in forward]
        else:
            outs.append("part" if self.carry else f"exit{backward[-1]}")
        self.vmem_out = outs
        if backward:
            outs += [f"grad{j}" for j in range(self.reach + 1)]

    def out_shape(self, name):
        side = self.side
        if name.startswith("grad"):
            shape = (self.grad_rows + (EXTRA if self.carry else 0), side)
        elif name == "part":
            shape = (2 * self.modes * side, side)
        elif name.startswith("crop"):
            shape = (self.windows, 2, side, side)
        else:
            shape = (self.windows, self.modes, 2, side, side)
        return jax.ShapeDtypeStruct(shape, jnp.float32)

    def __call__(self, values):
        inputs = ["offsets"] + self.vmem_in
        outputs = self.vmem_out
        args = [values[name] for name in inputs]
        shapes = [self.out_shape(name) for name in outputs]
        smem, vmem = (pl.BlockSpec(memory_space=space) for space in (pltpu.SMEM, pltpu.VMEM))
        outs = pl.pallas_call(
            self.kernel,
            out_shape=shapes,
            in_specs=[smem] + [vmem] * len(self.vmem_in),
            out_specs=[vmem] * len(self.vmem_out),
            cost_estimate=pl.CostEstimate(flops=0, bytes_accessed=0, transcendentals=0),
            compiler_params=pltpu.CompilerParams(vmem_limit_bytes=VMEM_BYTES),
        )(*args)
        return dict(zip(outputs, outs))

    def kernel(self, *refs):
        names = ["offsets"] + self.vmem_in + self.vmem_out
        r = dict(zip(names, refs))
        side, rows_here, modes, group = self.side, self.rows_here, self.modes, self.group
        forward, backward = self.forward, self.backward
        step, step_conj, transform, transform_conj = (
            (r["tables"][i, 0], r["tables"][i, 1]) for i in range(4)
        )
        me = lax.axis_index("tile")
        parity, moved = me % 2, moved_here(me)
        blocks = self.cols // LANES

        if self.carry:
            index = lax.broadcasted_iota(jnp.int32, (EXTRA, side), 0)
            carried = jnp.zeros((EXTRA, side), jnp.int32)
            for w in range(self.windows):
                carried = jnp.where(index == w, r["offsets"][1, w], carried)
            for j in range(1, self.reach + 1):
                r[f"grad{j}"][pl.ds(self.grad_rows, EXTRA)] = carried.astype(jnp.float32)
            r["part"][...] = jnp.zeros(r["part"].shape, jnp.float32)
        def start(w):
            row, col = r["offsets"][0, w], r["offsets"][1, w]
            block = col // LANES
            after = jnp.where(block + 1 == blocks, 0, block + 1)
            near, far = (pl.ds(pl.multiple_of(b * LANES, LANES), LANES) for b in (block, after))
            lane = col % LANES
            below = lax.broadcasted_iota(jnp.int32, (rows_here, side), 0) >= row
            here = jnp.where(below, 1, 0) != moved
            wraps = lax.broadcasted_iota(jnp.int32, (rows_here, side), 1) < lane
            return row, lane, near, far, here, wraps

        def crop(s, place):
            _, _, near, far, here, wraps = place

            def columns(name, c):
                tile = r[name].at[pl.ds((2 * s + c) * rows_here, rows_here)]
                return jnp.where(wraps, tile[:, far], tile[:, near])

            def plane(c):
                first = jnp.where(here, columns("own", c), columns("edge", c))
                outer = jnp.where(parity == moved, columns("own_mate", c), columns("edge_mate", c))
                inner = columns("partner_mate", c)
                pair = [jnp.where(parity == 0, a, b) for a, b in ((outer, inner), (inner, outer))]
                return jnp.concatenate([first, pair[0], columns("partner", c), pair[1]], axis=0)

            return (plane(0), plane(1))

        def keep(w, i, place, grad):
            here = place[4]
            for c in range(2):
                at = rows_at(((w * len(backward) + i) * 2 + c), rows_here)
                rows = [grad[c][j * rows_here : (j + 1) * rows_here] for j in range(self.reach)]
                r["grad0"][at] = jnp.where(here, rows[0], 0.0)
                r["grad1"][at] = jnp.where(here, 0.0, rows[0])
                r["grad2"][at] = rows[2]
                r["grad3"][at] = jnp.where(parity == 0, rows[3], rows[1])
                r["grad4"][at] = jnp.where(parity == 0, rows[1], rows[3])

        def turn(value, row, lane):
            return pltpu.roll(pltpu.roll(value, row, 0), lane, 1)

        def load(ref, w):
            return [tuple(ref[w, m, c] for c in range(2)) for m in range(modes)]

        def store(ref, w, waves):
            for m in range(modes):
                for c in range(2):
                    ref[w, m, c] = waves[m][c]

        def entry(w, s, place):
            if s > 0:
                return load(r[f"psi{s}"], w)
            return [
                tuple(turn(r["probe"][m, c], place[0], place[1]) for c in range(2)) for m in range(modes)
            ]

        def visit(index, carry):
            ids = [index * group + k for k in range(group)]
            turns = list(enumerate(ids))
            places = [start(w) for w in ids]
            crops, waves = {}, {}
            for k, w in turns:
                for s in forward:
                    crops[k, s] = crop(s, places[k])
                for s in backward:
                    if s not in forward:
                        crops[k, s] = tuple(r[f"crop{s}"][w, c] for c in range(2))
                        waves[k, s] = entry(w, s, places[k])
                for s in forward[:1]:
                    waves[k, s] = entry(w, s, places[k])
                if not backward:
                    for s in forward:
                        for c in range(2):
                            r[f"crop{s}"][w, c] = crops[k, s][c]
            for s in forward:
                exits = [[times(crops[k, s], wave) for wave in waves[k, s]] for k, w in turns]
                if self.far and s == forward[-1]:
                    break
                for k, w in turns:
                    waves[k, s + 1] = both_sides(exits[k], step, step_conj)
                    if not backward:
                        store(r[f"psi{s + 1}"], w, waves[k, s + 1])
            if self.far:
                exits = [both_sides(out, transform, transform_conj) for out in exits]
                for k, w in turns:
                    intensity = sum(re * re + im * im for re, im in exits[k])
                    scale = 1.0 - r["amplitude"][rows_at(w, side)] * lax.rsqrt(intensity + INTENSITY_SHIFT)
                    exits[k] = [(re * scale, im * scale) for re, im in exits[k]]
                exits = [both_sides(out, transform_conj, transform) for out in exits]
            elif backward:
                exits = [load(r[f"exit{backward[0] + 1}"], w) for w in ids]
            for i, s in enumerate(backward):
                if not (self.far and i == 0):
                    exits = [both_sides(out, step_conj, step) for out in exits]
                for k, w in turns:
                    terms = [conj_times(wave, out) for wave, out in zip(waves[k, s], exits[k])]
                    keep(w, s - backward[-1], places[k], [sum(term[c] for term in terms) for c in range(2)])
                    exits[k] = [conj_times(crops[k, s], out) for out in exits[k]]
            if self.carry:
                for k, (row, lane, *_) in enumerate(places):
                    for m in range(modes):
                        for c in range(2):
                            back = turn(exits[k][m][c], (side - row) % side, (side - lane) % side)
                            r["part"][pl.ds((2 * m + c) * side, side)] += back
            elif backward:
                for k, w in turns:
                    store(r[f"exit{backward[-1]}"], w, exits[k])
            return carry

        if self.windows == group:
            visit(0, 0)
        else:
            lax.fori_loop(0, self.windows // group, visit, 0)


def give_kernel(windows, count, col_ref, *refs):
    pieces, base, out_ref = refs[:count], refs[count:-1], refs[-1]
    planes, rows, cols = out_ref.shape
    blocks = cols // LANES
    lanes = lax.broadcasted_iota(jnp.int32, (1, 1, LANES), 2)
    out_ref[...] = base[0][...] if base else jnp.zeros(out_ref.shape, jnp.float32)
    for k, piece in enumerate(pieces):
        for w in range(windows):
            col = col_ref[k, w]
            block, lane = col // LANES, col % LANES
            after = jnp.where(block + 1 == blocks, 0, block + 1)
            near, far = (pl.ds(pl.multiple_of(b * LANES, LANES), LANES) for b in (block, after))
            value = piece[pl.ds(w * planes * rows, planes * rows)].reshape(planes, rows, LANES)
            wraps = lanes < lane
            out_ref[:, :, near] += jnp.where(wraps, 0.0, value)
            out_ref[:, :, far] += jnp.where(wraps, value, 0.0)


def give(windows, columns, pieces, shape, base=(), estimate=0):
    smem, vmem = (pl.BlockSpec(memory_space=space) for space in (pltpu.SMEM, pltpu.VMEM))
    return pl.pallas_call(
        functools.partial(give_kernel, windows, len(pieces)),
        out_shape=jax.ShapeDtypeStruct(shape, jnp.float32),
        in_specs=[smem] + [vmem] * (len(pieces) + len(base)),
        out_specs=vmem,
        cost_estimate=pl.CostEstimate(flops=estimate, bytes_accessed=0, transcendentals=0),
        compiler_params=pltpu.CompilerParams(vmem_limit_bytes=VMEM_BYTES),
    )(jnp.stack(columns), *pieces, *base)


def fetch(*arrays):
    def kernel(*refs):
        count = len(arrays)
        sources, targets, done = refs[:count], refs[count : 2 * count], refs[-1]
        copies = [pltpu.make_async_copy(*refs, done.at[i]) for i, refs in enumerate(zip(sources, targets))]
        for copy in copies:
            copy.start()
        for copy in copies:
            copy.wait()

    anywhere, vmem = pl.BlockSpec(memory_space=pltpu.HBM), pl.BlockSpec(memory_space=pltpu.VMEM)
    return pl.pallas_call(
        kernel,
        out_shape=[jax.ShapeDtypeStruct(x.shape, x.dtype) for x in arrays],
        in_specs=[anywhere] * len(arrays),
        out_specs=[vmem] * len(arrays),
        scratch_shapes=[pltpu.SemaphoreType.DMA((len(arrays),))],
        compiler_params=pltpu.CompilerParams(vmem_limit_bytes=VMEM_BYTES),
    )(*arrays)


def offsets_of(measured):
    def kernel(source, target):
        target[...] = source[pl.ds(source.shape[0] - EXTRA, EXTRA)].astype(jnp.int32)

    vmem = pl.BlockSpec(memory_space=pltpu.VMEM)
    return pl.pallas_call(
        kernel,
        out_shape=jax.ShapeDtypeStruct((EXTRA, measured.shape[1]), jnp.int32),
        in_specs=[vmem],
        out_specs=vmem,
        cost_estimate=pl.CostEstimate(flops=20_000_000_000, bytes_accessed=40_000_000, transcendentals=0),
        compiler_params=pltpu.CompilerParams(vmem_limit_bytes=VMEM_BYTES),
    )(measured)


def rows_at(block, size):
    first = block * size
    return pl.ds(first if isinstance(first, int) else pl.multiple_of(first, size), size)


def moved_here(tile):
    return tile // 2 % 2


def swap(value, bits):
    count = lax.axis_size("tile")
    return lax.ppermute(value, "tile", [(i, i ^ bits) for i in range(count)])


def sum_over_tiles(total):
    bit = 8
    while bit < lax.axis_size("tile"):
        total = total + swap(total, bit)
        bit *= 2
    return total


def on_device(slices, probe_modes, row_offset, col_offset, amplitude):
    modes, _, side, _ = probe_modes.shape
    slice_count, _, rows_here, cols = slices.shape
    windows = row_offset.shape[0]
    count = lax.axis_size("tile")
    reach = side // rows_here
    assert side == LANES and side % rows_here == 0 and cols % LANES == 0
    assert reach == 4 and count % reach == 0 and count & (count - 1) == 0
    home = [(t + reach) % count if moved_here(t) else t for t in range(count)]
    to_edge = [(t, home[t]) if moved_here(t) else ((t + reach) % count, t) for t in range(count)]
    from_edge = [(b, a) for a, b in to_edge]
    even = lax.axis_index("tile") % 2 == 0
    sizes = (windows, modes, side, rows_here, cols)

    def send(value, pairs_there):
        return lax.ppermute(value, "tile", pairs_there)


    def return_route(even_step, odd_step):
        return [(home[t], (t + (odd_step if t % 2 else even_step)) % count) for t in range(count)]

    flat = slices.reshape(slice_count * 2 * rows_here, cols)
    to_home = list(enumerate(home))
    partner, edge, own_mate = swap(flat, 2), send(flat, to_edge), swap(flat, 1)
    fetched = fetch(flat, probe_modes, jnp.asarray(tables_of(side)))
    partner, *fetched = lax.optimization_barrier((partner, *fetched))
    carried = jnp.stack([row_offset, col_offset]).astype(jnp.float32)
    carried = jnp.pad(carried, ((0, EXTRA - 2), (0, side - windows)))
    measured = jnp.concatenate([amplitude.reshape(windows * side, side), carried])
    measured = send(measured, to_home)
    offsets = offsets_of(measured)
    partner_mate, edge_mate = swap(partner, 1), swap(edge, 1)
    values = {
        "own": fetched[0],
        "probe": fetched[1],
        "tables": fetched[2],
        "offsets": offsets,
        "own_mate": own_mate,
        "partner": partner,
        "partner_mate": partner_mate,
        "edge": edge,
        "edge_mate": edge_mate,
        "amplitude": measured,
    }
    chunk = list(range(slice_count))
    result = Stage(chunk, True, chunk[::-1], sizes)(values)

    part = result["part"] + swap(result["part"], 2)
    lower, upper = part[: modes * side], part[modes * side :]
    total = jnp.where(even, lower, upper) + swap(jnp.where(even, upper, lower), 1)
    pieces = [result[f"grad{j}"] for j in range(reach + 1)]
    total, outer = lax.optimization_barrier((total, pieces[4]))
    total = total + swap(total, 4)
    early = [pieces[0], send(pieces[1], from_edge), send(pieces[2], return_route(2, 2))]
    late = [send(pieces[3], return_route(3, 1))]
    total, *early = lax.optimization_barrier((total, *early))
    late.append(send(outer, return_route(1, 3)))

    def columns_of(piece):
        return piece[-EXTRA:][:windows, 0].astype(jnp.int32)

    shape = (2 * slice_count, rows_here, cols)
    total, *early = lax.optimization_barrier((sum_over_tiles(total), *early, late.pop(0)))
    columns = [offsets[1, :windows]] + [columns_of(piece) for piece in early[1:]]
    own_grad = give(windows, columns, early, shape, estimate=0)
    total, own_grad, *late = lax.optimization_barrier((total, own_grad, *late))
    rest = swap(total, 1)
    own_grad = give(windows, [columns_of(piece) for piece in late], late, shape, [own_grad])
    own_grad = own_grad.reshape(slices.shape)
    probe_grad = jnp.where(even, jnp.concatenate([total, rest]), jnp.concatenate([rest, total]))
    return own_grad, probe_grad.reshape(probe_modes.shape)


def solution(mesh):
    placed = (
        P(None, None, ("scan", "tile"), None),
        P("scan", None, None, None),
        P(("scan", "tile")),
        P(("scan", "tile")),
        P(("scan", "tile"), None, None),
    )
    return jax.shard_map(
        on_device,
        mesh=mesh,
        in_specs=placed,
        out_specs=(P(None, None, ("scan", "tile"), None), P("scan", None, None, None)),
        check_vma=False,
    )
```

```python
import functools
import math

import numpy as np
import ml_dtypes
import jax
import jax.numpy as jnp
from jax import lax
from jax.experimental import pallas as pl
from jax.experimental.pallas import tpu as pltpu
from jax.sharding import PartitionSpec as P

INTENSITY_SHIFT = 0.5
FRESNEL = 0.75
LANES = 128
VMEM_BYTES = 20 * 1024 * 1024
EXTRA = 8


def pairs(value):
    first = value.astype(ml_dtypes.bfloat16)
    second = (value - first.astype(np.float64)).astype(ml_dtypes.bfloat16)
    return np.stack([first, second])


def real_form(matrix):
    return np.block([[matrix.real, matrix.imag], [-matrix.imag, matrix.real]])


def tables_of(window_side):
    steps = np.arange(window_side)
    angles = -2.0 * math.pi / window_side * (steps[:, None] * steps[None, :] % window_side)
    transform = np.exp(1j * angles) / math.sqrt(window_side)
    freqs = (steps + window_side // 2) % window_side - window_side // 2
    phase = np.exp(-1j * math.pi * FRESNEL * freqs**2 / (window_side / 2.0) ** 2)
    step = transform.conj() @ (phase[:, None] * transform)
    forms = [real_form(m) for m in (step, step.conj(), transform, transform.conj())]
    return np.stack([pairs(form) for form in forms])


def halves(value):
    first = value.astype(jnp.bfloat16)
    return first, (value - first.astype(jnp.float32)).astype(jnp.bfloat16)


def product(left, right):
    return jnp.dot(left, right, preferred_element_type=jnp.float32)


def right_apply(field, table):
    first, second = halves(field)
    return product(first, table[0]) + (product(second, table[0]) + product(first, table[1]))


def left_apply(table, field):
    first, second = halves(field)
    return product(table[0], first) + (product(table[0], second) + product(table[1], first))


def both_sides(waves, right_table, left_table):
    side = waves[0][0].shape[0]
    rows = jnp.concatenate([jnp.concatenate(wave, axis=1) for wave in waves], axis=0)
    half = right_apply(rows, right_table)
    count = len(waves)
    parts = [
        jnp.concatenate(
            [half[m * side : (m + 1) * side, c * side : (c + 1) * side] for m in range(count)], axis=1
        )
        for c in range(2)
    ]
    full = left_apply(left_table, jnp.concatenate(parts, axis=0))
    return [
        tuple(full[c * side : (c + 1) * side, m * side : (m + 1) * side] for c in range(2))
        for m in range(count)
    ]


def times(a, b):
    return (a[0] * b[0] - a[1] * b[1], a[0] * b[1] + a[1] * b[0])


def conj_times(a, b):
    return (a[0] * b[0] + a[1] * b[1], a[0] * b[1] - a[1] * b[0])


class Stage:
    def __init__(self, forward, far, backward, sizes):
        self.forward, self.far, self.backward = forward, far, backward
        self.windows, self.modes, self.side, self.rows_here, self.cols = sizes
        self.reach = self.side // self.rows_here
        self.carry = 0 in backward
        self.grad_rows = self.windows * len(backward) * 2 * self.rows_here
        self.group = math.gcd(self.windows, 4)
        loaded = set(backward) - set(forward)
        waves = loaded | set(forward[:1])
        vmem = ["tables"]
        vmem += ["probe"] if 0 in waves else []
        vmem += ["amplitude"] if far else []
        vmem += [f"psi{s}" for s in sorted(waves) if s > 0] + [f"crop{s}" for s in sorted(loaded)]
        vmem += [] if far else [f"exit{s + 1}" for s in backward[:1]]
        if forward:
            vmem += ["own", "own_mate", "partner", "partner_mate", "edge", "edge_mate"]
        self.vmem_in = vmem
        outs = [f"grad{j}" for j in range(self.reach + 1)] if backward else []
        if not backward:
            outs += [f"psi{s + 1}" for s in forward] + [f"crop{s}" for s in forward]
        else:
            outs.append("part" if self.carry else f"exit{backward[-1]}")
        self.vmem_out = outs
        if backward:
            outs += [f"grad{j}" for j in range(self.reach + 1)]

    def out_shape(self, name):
        side = self.side
        if name.startswith("grad"):
            shape = (self.grad_rows + (EXTRA if self.carry else 0), side)
        elif name == "part":
            shape = (2 * self.modes * side, side)
        elif name.startswith("crop"):
            shape = (self.windows, 2, side, side)
        else:
            shape = (self.windows, self.modes, 2, side, side)
        return jax.ShapeDtypeStruct(shape, jnp.float32)

    def __call__(self, values):
        inputs = ["offsets"] + self.vmem_in
        outputs = self.vmem_out
        args = [values[name] for name in inputs]
        shapes = [self.out_shape(name) for name in outputs]
        smem, vmem = (pl.BlockSpec(memory_space=space) for space in (pltpu.SMEM, pltpu.VMEM))
        outs = pl.pallas_call(
            self.kernel,
            out_shape=shapes,
            in_specs=[smem] + [vmem] * len(self.vmem_in),
            out_specs=[vmem] * len(self.vmem_out),
            cost_estimate=pl.CostEstimate(flops=0, bytes_accessed=0, transcendentals=0),
            compiler_params=pltpu.CompilerParams(vmem_limit_bytes=VMEM_BYTES),
        )(*args)
        return dict(zip(outputs, outs))

    def kernel(self, *refs):
        names = ["offsets"] + self.vmem_in + self.vmem_out
        r = dict(zip(names, refs))
        side, rows_here, modes, group = self.side, self.rows_here, self.modes, self.group
        forward, backward = self.forward, self.backward
        step, step_conj, transform, transform_conj = (
            (r["tables"][i, 0], r["tables"][i, 1]) for i in range(4)
        )
        me = lax.axis_index("tile")
        parity, moved = me % 2, moved_here(me)
        blocks = self.cols // LANES

        if self.carry:
            index = lax.broadcasted_iota(jnp.int32, (EXTRA, side), 0)
            carried = jnp.zeros((EXTRA, side), jnp.int32)
            for w in range(self.windows):
                carried = jnp.where(index == w, r["offsets"][1, w], carried)
            for j in range(1, self.reach + 1):
                r[f"grad{j}"][pl.ds(self.grad_rows, EXTRA)] = carried.astype(jnp.float32)
            r["part"][...] = jnp.zeros(r["part"].shape, jnp.float32)
        def start(w):
            row, col = r["offsets"][0, w], r["offsets"][1, w]
            block = col // LANES
            after = jnp.where(block + 1 == blocks, 0, block + 1)
            near, far = (pl.ds(pl.multiple_of(b * LANES, LANES), LANES) for b in (block, after))
            lane = col % LANES
            below = lax.broadcasted_iota(jnp.int32, (rows_here, side), 0) >= row
            here = jnp.where(below, 1, 0) != moved
            wraps = lax.broadcasted_iota(jnp.int32, (rows_here, side), 1) < lane
            return row, lane, near, far, here, wraps

        def crop(s, place):
            _, _, near, far, here, wraps = place

            def columns(name, c):
                tile = r[name].at[pl.ds((2 * s + c) * rows_here, rows_here)]
                return jnp.where(wraps, tile[:, far], tile[:, near])

            def plane(c):
                first = jnp.where(here, columns("own", c), columns("edge", c))
                outer = jnp.where(parity == moved, columns("own_mate", c), columns("edge_mate", c))
                inner = columns("partner_mate", c)
                pair = [jnp.where(parity == 0, a, b) for a, b in ((outer, inner), (inner, outer))]
                return jnp.concatenate([first, pair[0], columns("partner", c), pair[1]], axis=0)

            return (plane(0), plane(1))

        def keep(w, i, place, grad):
            here = place[4]
            for c in range(2):
                at = rows_at(((w * len(backward) + i) * 2 + c), rows_here)
                rows = [grad[c][j * rows_here : (j + 1) * rows_here] for j in range(self.reach)]
                r["grad0"][at] = jnp.where(here, rows[0], 0.0)
                r["grad1"][at] = jnp.where(here, 0.0, rows[0])
                r["grad2"][at] = rows[2]
                r["grad3"][at] = jnp.where(parity == 0, rows[3], rows[1])
                r["grad4"][at] = jnp.where(parity == 0, rows[1], rows[3])

        def turn(value, row, lane):
            return pltpu.roll(pltpu.roll(value, row, 0), lane, 1)

        def load(ref, w):
            return [tuple(ref[w, m, c] for c in range(2)) for m in range(modes)]

        def store(ref, w, waves):
            for m in range(modes):
                for c in range(2):
                    ref[w, m, c] = waves[m][c]

        def entry(w, s, place):
            if s > 0:
                return load(r[f"psi{s}"], w)
            return [
                tuple(turn(r["probe"][m, c], place[0], place[1]) for c in range(2)) for m in range(modes)
            ]

        def visit(index, carry):
            ids = [index * group + k for k in range(group)]
            turns = list(enumerate(ids))
            places = [start(w) for w in ids]
            crops, waves = {}, {}
            for k, w in turns:
                for s in forward:
                    crops[k, s] = crop(s, places[k])
                for s in backward:
                    if s not in forward:
                        crops[k, s] = tuple(r[f"crop{s}"][w, c] for c in range(2))
                        waves[k, s] = entry(w, s, places[k])
                for s in forward[:1]:
                    waves[k, s] = entry(w, s, places[k])
                if not backward:
                    for s in forward:
                        for c in range(2):
                            r[f"crop{s}"][w, c] = crops[k, s][c]
            for s in forward:
                exits = [[times(crops[k, s], wave) for wave in waves[k, s]] for k, w in turns]
                if self.far and s == forward[-1]:
                    break
                for k, w in turns:
                    waves[k, s + 1] = both_sides(exits[k], step, step_conj)
                    if not backward:
                        store(r[f"psi{s + 1}"], w, waves[k, s + 1])
            if self.far:
                exits = [both_sides(out, transform, transform_conj) for out in exits]
                for k, w in turns:
                    intensity = sum(re * re + im * im for re, im in exits[k])
                    scale = 1.0 - r["amplitude"][rows_at(w, side)] * lax.rsqrt(intensity + INTENSITY_SHIFT)
                    exits[k] = [(re * scale, im * scale) for re, im in exits[k]]
                exits = [both_sides(out, transform_conj, transform) for out in exits]
            elif backward:
                exits = [load(r[f"exit{backward[0] + 1}"], w) for w in ids]
            for i, s in enumerate(backward):
                if not (self.far and i == 0):
                    exits = [both_sides(out, step_conj, step) for out in exits]
                for k, w in turns:
                    terms = [conj_times(wave, out) for wave, out in zip(waves[k, s], exits[k])]
                    keep(w, s - backward[-1], places[k], [sum(term[c] for term in terms) for c in range(2)])
                    exits[k] = [conj_times(crops[k, s], out) for out in exits[k]]
            if self.carry:
                for k, (row, lane, *_) in enumerate(places):
                    for m in range(modes):
                        for c in range(2):
                            back = turn(exits[k][m][c], (side - row) % side, (side - lane) % side)
                            r["part"][pl.ds((2 * m + c) * side, side)] += back
            elif backward:
                for k, w in turns:
                    store(r[f"exit{backward[-1]}"], w, exits[k])
            return carry

        if self.windows == group:
            visit(0, 0)
        else:
            lax.fori_loop(0, self.windows // group, visit, 0)


def give_kernel(windows, count, col_ref, *refs):
    pieces, base, out_ref = refs[:count], refs[count:-1], refs[-1]
    planes, rows, cols = out_ref.shape
    blocks = cols // LANES
    lanes = lax.broadcasted_iota(jnp.int32, (1, 1, LANES), 2)
    out_ref[...] = base[0][...] if base else jnp.zeros(out_ref.shape, jnp.float32)
    for k, piece in enumerate(pieces):
        for w in range(windows):
            col = col_ref[k, w]
            block, lane = col // LANES, col % LANES
            after = jnp.where(block + 1 == blocks, 0, block + 1)
            near, far = (pl.ds(pl.multiple_of(b * LANES, LANES), LANES) for b in (block, after))
            value = piece[pl.ds(w * planes * rows, planes * rows)].reshape(planes, rows, LANES)
            wraps = lanes < lane
            out_ref[:, :, near] += jnp.where(wraps, 0.0, value)
            out_ref[:, :, far] += jnp.where(wraps, value, 0.0)


def give(windows, columns, pieces, shape, base=(), estimate=0):
    smem, vmem = (pl.BlockSpec(memory_space=space) for space in (pltpu.SMEM, pltpu.VMEM))
    return pl.pallas_call(
        functools.partial(give_kernel, windows, len(pieces)),
        out_shape=jax.ShapeDtypeStruct(shape, jnp.float32),
        in_specs=[smem] + [vmem] * (len(pieces) + len(base)),
        out_specs=vmem,
        cost_estimate=pl.CostEstimate(flops=estimate, bytes_accessed=0, transcendentals=0),
        compiler_params=pltpu.CompilerParams(vmem_limit_bytes=VMEM_BYTES),
    )(jnp.stack(columns), *pieces, *base)


def fetch(*arrays):
    def kernel(*refs):
        count = len(arrays)
        sources, targets, done = refs[:count], refs[count : 2 * count], refs[-1]
        copies = [pltpu.make_async_copy(*refs, done.at[i]) for i, refs in enumerate(zip(sources, targets))]
        for copy in copies:
            copy.start()
        for copy in copies:
            copy.wait()

    anywhere, vmem = pl.BlockSpec(memory_space=pltpu.HBM), pl.BlockSpec(memory_space=pltpu.VMEM)
    return pl.pallas_call(
        kernel,
        out_shape=[jax.ShapeDtypeStruct(x.shape, x.dtype) for x in arrays],
        in_specs=[anywhere] * len(arrays),
        out_specs=[vmem] * len(arrays),
        scratch_shapes=[pltpu.SemaphoreType.DMA((len(arrays),))],
        compiler_params=pltpu.CompilerParams(vmem_limit_bytes=VMEM_BYTES),
    )(*arrays)


def offsets_of(measured):
    def kernel(source, target):
        target[...] = source[pl.ds(source.shape[0] - EXTRA, EXTRA)].astype(jnp.int32)

    vmem = pl.BlockSpec(memory_space=pltpu.VMEM)
    return pl.pallas_call(
        kernel,
        out_shape=jax.ShapeDtypeStruct((EXTRA, measured.shape[1]), jnp.int32),
        in_specs=[vmem],
        out_specs=vmem,
        cost_estimate=pl.CostEstimate(flops=20_000_000_000, bytes_accessed=40_000_000, transcendentals=0),
        compiler_params=pltpu.CompilerParams(vmem_limit_bytes=VMEM_BYTES),
    )(measured)


def rows_at(block, size):
    first = block * size
    return pl.ds(first if isinstance(first, int) else pl.multiple_of(first, size), size)


def moved_here(tile):
    return tile // 2 % 2


def swap(value, bits):
    count = lax.axis_size("tile")
    return lax.ppermute(value, "tile", [(i, i ^ bits) for i in range(count)])


def sum_over_tiles(total):
    bit = 8
    while bit < lax.axis_size("tile"):
        total = total + swap(total, bit)
        bit *= 2
    return total


def on_device(slices, probe_modes, row_offset, col_offset, amplitude):
    modes, _, side, _ = probe_modes.shape
    slice_count, _, rows_here, cols = slices.shape
    windows = row_offset.shape[0]
    count = lax.axis_size("tile")
    reach = side // rows_here
    assert side == LANES and side % rows_here == 0 and cols % LANES == 0
    assert reach == 4 and count % reach == 0 and count & (count - 1) == 0
    home = [(t + reach) % count if moved_here(t) else t for t in range(count)]
    to_edge = [(t, home[t]) if moved_here(t) else ((t + reach) % count, t) for t in range(count)]
    from_edge = [(b, a) for a, b in to_edge]
    even = lax.axis_index("tile") % 2 == 0
    sizes = (windows, modes, side, rows_here, cols)

    def send(value, pairs_there):
        return lax.ppermute(value, "tile", pairs_there)


    def return_route(even_step, odd_step):
        return [(home[t], (t + (odd_step if t % 2 else even_step)) % count) for t in range(count)]

    flat = slices.reshape(slice_count * 2 * rows_here, cols)
    to_home = list(enumerate(home))
    partner, edge, own_mate = swap(flat, 2), send(flat, to_edge), swap(flat, 1)
    fetched = fetch(flat, probe_modes, jnp.asarray(tables_of(side)))
    partner, *fetched = lax.optimization_barrier((partner, *fetched))
    carried = jnp.stack([row_offset, col_offset]).astype(jnp.float32)
    carried = jnp.pad(carried, ((0, EXTRA - 2), (0, side - windows)))
    measured = jnp.concatenate([amplitude.reshape(windows * side, side), carried])
    measured = send(measured, to_home)
    offsets = offsets_of(measured)
    partner_mate, edge_mate = swap(partner, 1), swap(edge, 1)
    values = {
        "own": fetched[0],
        "probe": fetched[1],
        "tables": fetched[2],
        "offsets": offsets,
        "own_mate": own_mate,
        "partner": partner,
        "partner_mate": partner_mate,
        "edge": edge,
        "edge_mate": edge_mate,
        "amplitude": measured,
    }
    chunk = list(range(slice_count))
    result = Stage(chunk, True, chunk[::-1], sizes)(values)

    part = result["part"] + swap(result["part"], 2)
    lower, upper = part[: modes * side], part[modes * side :]
    total = jnp.where(even, lower, upper) + swap(jnp.where(even, upper, lower), 1)
    pieces = [result[f"grad{j}"] for j in range(reach + 1)]
    total, outer = lax.optimization_barrier((total, pieces[4]))
    total = total + swap(total, 4)
    first = send(pieces[2], return_route(2, 2))
    early = [pieces[0], send(pieces[1], from_edge), first]
    late = [send(pieces[3], return_route(3, 1))]
    total, *early = lax.optimization_barrier((total, *early))
    late.append(send(outer, return_route(1, 3)))

    def columns_of(piece):
        return piece[-EXTRA:][:windows, 0].astype(jnp.int32)

    shape = (2 * slice_count, rows_here, cols)
    total, *early = lax.optimization_barrier((sum_over_tiles(total), *early, late.pop(0)))
    columns = [offsets[1, :windows]] + [columns_of(piece) for piece in early[1:]]
    own_grad = give(windows, columns, early, shape, estimate=0)
    total, own_grad, *late = lax.optimization_barrier((total, own_grad, *late))
    rest = swap(total, 1)
    own_grad = give(windows, [columns_of(piece) for piece in late], late, shape, [own_grad])
    own_grad = own_grad.reshape(slices.shape)
    probe_grad = jnp.where(even, jnp.concatenate([total, rest]), jnp.concatenate([rest, total]))
    return own_grad, probe_grad.reshape(probe_modes.shape)


def solution(mesh):
    placed = (
        P(None, None, ("scan", "tile"), None),
        P("scan", None, None, None),
        P(("scan", "tile")),
        P(("scan", "tile")),
        P(("scan", "tile"), None, None),
    )
    return jax.shard_map(
        on_device,
        mesh=mesh,
        in_specs=placed,
        out_specs=(P(None, None, ("scan", "tile"), None), P("scan", None, None, None)),
        check_vma=False,
    )
```
